128 devices in a mesh: gx: 32 (over x, z_lo, y), gy: 4 (over z_hi, core).
Axes of the slice: x: 4, y: 4, z: 4 (z_hi: 2, z_lo: 2; z = z_hi * 2 + z_lo), core: 2. Of those that a mesh axis runs over, the one named last changes fastest.
Arguments:
- populations: float32 [19, 256, 16384], P(None, 'gx', 'gy'), may hold values from 0 to 1, as said below
- node_cell: int32 [49152, 256], P(('gx', 'gy')), may hold values from 0 to 32767
- node_weight: bfloat16 [49152, 256], P(('gx', 'gy')), may hold values from 0.19921875 to 2
- node_count: int32 [49152], P(('gx', 'gy')), may hold values from 1 to 256, 11010048 in all
- block_brick: int32 [49152, 1], P(('gx', 'gy')), may hold values from 0 to 127; in each aligned block of 384 rows (0 to 383, 384 to 767, ...) at most 4 rows name the same one
Outputs:
- flow_state: float32 [19, 256, 16384], P(None, 'gx', 'gy')
- solid_frac: float32 [256, 16384], P('gx', 'gy')
The draws below stay inside these ranges and needn't reach their ends.
Inputs may be any that keep to these rules, and one draw needn't show every extreme that they name: `block_brick`: no brick is named by more than 4 of the 384 blocks of one device (aligned blocks of 384 rows); some brick is named by exactly 4 of them. `populations`: each population lies between half and twice its lattice weight w_i.
All inputs are finite; a program needn't handle non-finite values. No bound on the sum of `node_count` on one device may be relied on, other than what follows from the above.
Results may differ from the reference program's by a relative error of at most 0.00095.
Values may be sent and summed in bfloat16 or wider, within the bound.
A program may use at most 192 MiB of HBM per device.

```python
import math
import jax
import jax.numpy as jnp
import numpy as np

BX = 8
BY = 64
NZ = 64
Q = 19
STEPS = 3
NODES = 256
CAP = 4
BLK = 384
BRICKS = 128
YBLOCKS = 49152
NX = 256
NY = 256
NYZ = 16384
N_GY = 4


def draw_populations(key, part):
    key = jax.random.fold_in(key, 7)
    weight_table = jnp.array([1.0 / 3.0] + [1.0 / 18.0] * 6 + [1.0 / 36.0] * 12, jnp.float32)[:, None, None]
    grid_shape = (Q, NX, NYZ)
    factor = jnp.exp(jax.random.uniform(key, grid_shape, jnp.float32, -math.log(2.0), math.log(2.0)))
    return (weight_table * factor).astype(jnp.float32)


def plant(entries, key, low, top_value):
    index_at = [jax.random.randint(jax.random.fold_in(key, axis), (), 0, length) for axis, length in enumerate(entries.shape)]
    longest = entries.shape.index(max(entries.shape))
    next_to = index_at[:longest] + [(index_at[longest] + 1) % entries.shape[longest]] + index_at[longest + 1:]
    return entries.at[tuple(index_at)].set(low).at[tuple(next_to)].set(top_value)


def shard_levels(rng, dims, pieces, smallest, high):
    loudness = 1.0
    for position, parts in pieces:
        heights = jax.random.uniform(jax.random.fold_in(jax.random.fold_in(rng, 6), position), (parts,), jnp.float32, smallest / len(pieces), high / len(pieces))
        loudness = loudness * jnp.repeat(jnp.exp(heights), dims[position] // parts).reshape((-1,) + (1,) * (len(dims) - 1 - position))
    return loudness


def profile(amount, total, most, lean):
    portions = [(1 << 20) // math.isqrt(grade ** lean) + 1 for grade in range(2, amount + 1)]
    rest, counts = total - most - (amount - 1), [1] * (amount - 1)
    while rest > 0:
        candidates = [i for i in range(amount - 1) if counts[i] < most]
        pool, left = sum([portions[i] for i in candidates]), rest
        for i in candidates:
            extra = min(most - counts[i], max(1, left * portions[i] // pool), rest)
            counts[i] = counts[i] + extra
            rest = rest - extra
    return np.array([most] + counts)


def ragged_sizes(rng, amount, total, limit, slope):
    if amount == 2:
        one = jax.random.randint(rng, (), max(1, total - limit), min(limit, total - 1) + 1)
        return jnp.stack([one, total - one])
    sizes = jnp.asarray(profile(amount, total, limit, slope), jnp.int32)
    couples = (amount - 1) // 2
    source_of, receiver = sizes[1:1 + 2 * couples:2], sizes[2:2 + 2 * couples:2]
    slack = jnp.minimum(source_of - 1, limit - receiver)
    moved = jax.random.randint(jax.random.fold_in(rng, 1), (couples,), 0, 1 << 20) % (slack + 1)
    sizes = sizes.at[1:1 + 2 * couples:2].set(source_of - moved).at[2:2 + 2 * couples:2].set(receiver + moved)
    return sizes[jax.random.permutation(jax.random.fold_in(rng, 2), amount)]


def assign_block(key, own, number, rows, amount, top, most, lean):
    sequence = jax.random.permutation(key, amount)
    crowded, usual = portions_of(amount, rows * top, most, lean, True), portions_of(amount, rows * top, most, lean, False)
    places = jnp.arange(amount)

    def named(lengths, turn):
        used = int((lengths > 0).sum())
        fixed = max(1, used // 4)
        moved = fixed + (places - fixed + turn * (used - fixed)) % max(1, amount - fixed)
        return jnp.zeros((amount,), jnp.int32).at[sequence[jnp.where(places < fixed, places, moved)]].set(jnp.asarray(lengths, jnp.int32))

    lengths = jnp.where(number % 4 == 0, named(crowded, number // 4), named(usual, number - number // 4 - 1))
    mixed = jax.random.permutation(jax.random.fold_in(own, 3), amount)
    source_of, receiver = mixed[0:amount // 2 * 2:2], mixed[1:amount // 2 * 2:2]
    slack = jnp.minimum(lengths[source_of] - 1, most - lengths[receiver]) // 2
    slack = jnp.where((source_of == sequence[0]) | (receiver == sequence[0]) | (lengths[receiver] == 0), 0, jnp.maximum(slack, 0))
    moved = jax.random.randint(jax.random.fold_in(own, 4), (amount // 2,), 0, 1 << 20) % (slack + 1)
    lengths = lengths.at[source_of].add(-moved).at[receiver].add(moved)
    labels = jnp.searchsorted(jnp.cumsum(lengths), jnp.arange(rows * top), side="right").astype(jnp.int32)
    listing = labels.reshape(top, rows).T
    listing = listing[jax.random.permutation(jax.random.fold_in(own, 1), rows)]
    turn = jax.random.randint(jax.random.fold_in(own, 2), (rows, 1), 0, top)
    return jnp.take_along_axis(listing, (jnp.arange(top)[None, :] + turn) % top, axis=1)


def portions_of(amount, total, limit, skew, full):
    portions = [(1 << 20) // math.isqrt(standing ** skew) + 1 for standing in range(1, amount + 1)]
    largest = limit if full else min(limit, max(-(-total // amount), total * portions[0] // sum(portions)))
    least = 1 if total - largest >= amount - 1 else 0
    holding, rest = [largest] + [least] * (amount - 1), total - largest - least * (amount - 1)
    while rest > 0:
        candidates = [i for i in range(1, amount) if holding[i] < largest] or [i for i in range(1, amount) if holding[i] < limit]
        pool, remaining = sum([portions[i] for i in candidates]), rest
        for i in candidates:
            more = min(limit - holding[i], max(1, remaining * portions[i] // pool), rest)
            holding[i] = holding[i] + more
            rest = rest - more
    return np.array(holding)


def setup_inputs(seed: int = 0) -> dict:
    arg_keys = jax.random.split(jax.random.key(seed), 6)
    populations = draw_populations(jax.random.fold_in(arg_keys[5], 71), 0)
    node_cell = plant(jax.random.randint(arg_keys[1], (YBLOCKS, NODES), 0, BX * BY * NZ), jax.random.fold_in(arg_keys[1], 1), 0, (BX * BY * NZ) - 1).astype(jnp.int32)
    node_weight = jnp.clip(jnp.exp(math.log(2.0) - 2.306499 * jax.random.uniform(arg_keys[2], (YBLOCKS, NODES), jnp.float32) ** shard_levels(arg_keys[2], (YBLOCKS, NODES), ((0, 128),), -0.2, 0.2)), 0.19921875, 2.0).astype(jnp.bfloat16)
    node_count = ragged_sizes(arg_keys[3], YBLOCKS, 7 * YBLOCKS * NODES // 8, NODES, 1).astype(jnp.int32)
    block_brick_keys = jax.random.split(jax.random.fold_in(arg_keys[4], 1), YBLOCKS // BLK)
    block_brick_turns = jax.random.permutation(jax.random.fold_in(arg_keys[4], 3), YBLOCKS // BLK)
    block_brick = jax.vmap(lambda own, number: assign_block(jax.random.fold_in(arg_keys[4], 2), own, number, BLK, BRICKS, 1, CAP, 2))(block_brick_keys, block_brick_turns).reshape((YBLOCKS, 1))
    return {"populations": populations, "node_cell": node_cell, "node_weight": node_weight, "node_count": node_count, "block_brick": block_brick}


lattice_velocities = ((0, 0, 0), (1, 0, 0), (-1, 0, 0), (0, 1, 0), (0, -1, 0), (0, 0, 1), (0, 0, -1),
                      (1, 1, 0), (-1, -1, 0), (1, -1, 0), (-1, 1, 0), (1, 0, 1), (-1, 0, -1),
                      (1, 0, -1), (-1, 0, 1), (0, 1, 1), (0, -1, -1), (0, 1, -1), (0, -1, 1))
opposite_of = (0, 2, 1, 4, 3, 6, 5, 8, 7, 10, 9, 12, 11, 14, 13, 16, 15, 18, 17)
lattice_weights = (1.0 / 3.0,) + (1.0 / 18.0,) * 6 + (1.0 / 36.0,) * 12
relax_rate = 1.0


def roll_within(values, offset):
    if offset == 0:
        return values
    z_position = jnp.arange(values.shape[-1]) % NZ
    shifted = jnp.roll(values, offset, axis=-1)
    wrapped = jnp.roll(values, offset - offset * NZ, axis=-1)
    edge_at = 0 if offset > 0 else NZ - 1
    return jnp.where(z_position == edge_at, wrapped, shifted)


def collide(incoming, solid):
    x_dir = jnp.array([entry[0] for entry in lattice_velocities], jnp.float32)[:, None, None]
    y_dir = jnp.array([entry[1] for entry in lattice_velocities], jnp.float32)[:, None, None]
    z_dir = jnp.array([entry[2] for entry in lattice_velocities], jnp.float32)[:, None, None]
    weight_col = jnp.array(lattice_weights, jnp.float32)[:, None, None]
    mass_density = jnp.sum(incoming, axis=0)
    velocity_x = jnp.sum(incoming * x_dir, axis=0) / mass_density
    velocity_y = jnp.sum(incoming * y_dir, axis=0) / mass_density
    velocity_z = jnp.sum(incoming * z_dir, axis=0) / mass_density
    projected = x_dir * velocity_x + y_dir * velocity_y + z_dir * velocity_z
    speed_sq = velocity_x * velocity_x + velocity_y * velocity_y + velocity_z * velocity_z
    equilibrium = weight_col * mass_density * (1.0 + 3.0 * projected + 4.5 * projected * projected - 1.5 * speed_sq)
    reversed_pops = incoming[np.array(opposite_of)]
    return (1.0 - solid) * (incoming + relax_rate * (equilibrium - incoming)) + solid * reversed_pops


def stream_periodic(collided):
    pulled = []
    for number, velocity in enumerate(lattice_velocities):
        moved_x = jnp.roll(collided[number], velocity[0], axis=0)
        moved_xy = jnp.roll(moved_x, velocity[1] * NZ, axis=1)
        pulled.append(roll_within(moved_xy, velocity[2]))
    return jnp.stack(pulled)


def solid_fraction(node_cell, node_weight, node_count, block_brick):
    target = block_brick[:, 0]
    brick_x = target // N_GY
    brick_y = target % N_GY
    local_x = node_cell // (BY * NZ)
    local_yz = node_cell % (BY * NZ)
    global_cell = (brick_x[:, None] * BX + local_x) * (NY * NZ) + brick_y[:, None] * (BY * NZ) + local_yz
    live_mask = jnp.arange(node_cell.shape[1], dtype=jnp.int32)[None, :] < node_count[:, None]
    contribution = jnp.where(live_mask, node_weight.astype(jnp.float32), jnp.zeros((), jnp.float32))
    density = jnp.zeros((NX * NY * NZ,), jnp.float32).at[global_cell.reshape(-1)].add(contribution.reshape(-1))
    density = density.reshape(NX, NY * NZ)
    return density / (1.0 + density)


def reference(populations, node_cell, node_weight, node_count, block_brick):
    solid_frac = solid_fraction(node_cell, node_weight, node_count, block_brick)
    current = populations
    for repeat in range(STEPS):
        current = stream_periodic(collide(current, solid_frac))
    return current, solid_frac
```

```python
import functools

import jax
import jax.numpy as jnp
import numpy as np
from jax import lax
from jax.experimental import pallas as pl
from jax.experimental.pallas import tpu as pltpu
from jax.sharding import PartitionSpec as P

NZ = 64
STEPS = 3
CAP = 4
LANES = 128
GROUP = 8
CHUNK = 16
WEIGHT_STEPS = 1024.0
REST_SCALE = 64.0
MESH = pl.DeviceIdType.MESH
NARROW = jnp.float8_e4m3fn


lattice_velocities = (
    (0, 0, 0),
    (1, 0, 0),
    (-1, 0, 0),
    (0, 1, 0),
    (0, -1, 0),
    (0, 0, 1),
    (0, 0, -1),
    (1, 1, 0),
    (-1, -1, 0),
    (1, -1, 0),
    (-1, 1, 0),
    (1, 0, 1),
    (-1, 0, -1),
    (1, 0, -1),
    (-1, 0, 1),
    (0, 1, 1),
    (0, -1, -1),
    (0, 1, -1),
    (0, -1, 1),
)
opposite_of = (0, 2, 1, 4, 3, 6, 5, 8, 7, 10, 9, 12, 11, 14, 13, 16, 15, 18, 17)
lattice_weights = (1.0 / 3.0,) + (1.0 / 18.0,) * 6 + (1.0 / 36.0,) * 12
relax_rate = 1.0


def extended(block, sides, width):
    for axis, dim in sides:
        count = lax.axis_size(axis)
        forward = [(i, i + 1) for i in range(count - 1)]
        forward.append((count - 1, 0))
        backward = [(target, source) for source, target in forward]
        low = lax.ppermute(
            lax.slice_in_dim(block, block.shape[dim] - width, None, axis=dim), axis, forward
        )
        high = lax.ppermute(lax.slice_in_dim(block, 0, width, axis=dim), axis, backward)
        block = jnp.concatenate([low, block, high], axis=dim)
    return block


def roll_within(values, offset):
    if offset == 0:
        return values
    z_position = jnp.arange(values.shape[-1]) % NZ
    shifted = jnp.roll(values, offset, axis=-1)
    wrapped = jnp.roll(values, offset - offset * NZ, axis=-1)
    edge_at = 0 if offset > 0 else NZ - 1
    return jnp.where(z_position == edge_at, wrapped, shifted)


def collide(incoming, solid):
    x_dir = jnp.array([entry[0] for entry in lattice_velocities], jnp.float32)[:, None, None]
    y_dir = jnp.array([entry[1] for entry in lattice_velocities], jnp.float32)[:, None, None]
    z_dir = jnp.array([entry[2] for entry in lattice_velocities], jnp.float32)[:, None, None]
    weight_col = jnp.array(lattice_weights, jnp.float32)[:, None, None]
    mass_density = jnp.sum(incoming, axis=0)
    velocity_x = jnp.sum(incoming * x_dir, axis=0) / mass_density
    velocity_y = jnp.sum(incoming * y_dir, axis=0) / mass_density
    velocity_z = jnp.sum(incoming * z_dir, axis=0) / mass_density
    projected = x_dir * velocity_x + y_dir * velocity_y + z_dir * velocity_z
    speed_sq = velocity_x * velocity_x + velocity_y * velocity_y + velocity_z * velocity_z
    equilibrium = (
        weight_col
        * mass_density
        * (1.0 + 3.0 * projected + 4.5 * projected * projected - 1.5 * speed_sq)
    )
    reversed_pops = incoming[np.array(opposite_of)]
    return (1.0 - solid) * (
        incoming + relax_rate * (equilibrium - incoming)
    ) + solid * reversed_pops


def stream_pull(collided):
    extent_x = collided.shape[1]
    extent_yz = collided.shape[2]
    pulled = []
    for number, velocity in enumerate(lattice_velocities):
        shift_x, shift_y, shift_z = velocity
        source = collided[
            number,
            1 - shift_x : extent_x - 1 - shift_x,
            (1 - shift_y) * NZ : extent_yz - (1 + shift_y) * NZ,
        ]
        pulled.append(roll_within(source, shift_z))
    return jnp.stack(pulled)


def brick_slots(me, bricks, target_ref, count_ref, cell_ref, weight_ref, operand):
    blocks, nodes = cell_ref.shape
    row = lax.broadcasted_iota(jnp.int32, (blocks, blocks), 0)
    col = lax.broadcasted_iota(jnp.int32, (blocks, blocks), 1)
    target_col = target_ref[...]
    brick = lax.broadcasted_iota(jnp.int32, (blocks, bricks), 1)
    matches = jnp.where(brick == target_col, 1.0, 0.0)
    before = jnp.where(col < row, 1.0, 0.0).astype(jnp.bfloat16)
    earlier = jnp.dot(before, matches.astype(jnp.bfloat16), preferred_element_type=jnp.float32)
    rank = jnp.sum(earlier * matches, axis=1, keepdims=True)
    slot_col = target_col.astype(jnp.float32) * CAP + rank
    slot_row = jnp.sum(jnp.where(row == col, slot_col, 0.0), axis=0, keepdims=True)
    count_row = count_ref[...].astype(jnp.float32)
    count_col = jnp.sum(jnp.where(row == col, count_row, 0.0), axis=1, keepdims=True)
    node = lax.broadcasted_iota(jnp.int32, (blocks, nodes), 1).astype(jnp.float32)
    live = node < count_col
    cell = cell_ref[...]
    high = ((cell >> 7) & 31) * 8 + (cell >> 12)
    low = cell & 127
    weight = jnp.where(live, weight_ref[...].astype(jnp.float32), 0.0)
    for part in range(2):
        lanes = slice(part * LANES, (part + 1) * LANES)
        for number, values in enumerate((high.astype(jnp.float32), low.astype(jnp.float32), weight)):
            at = (part * 3 + number) * LANES
            operand[:, at : at + LANES] = values[:, lanes].astype(jnp.bfloat16)
    return slot_row


def send_chunk(me, bricks, along_y, chunk, slot_row, operand, outgoing, arrived, sent_sem, arrived_sem):
    rows = CHUNK * 8
    place = lax.broadcasted_iota(jnp.int32, (rows, 1), 0)
    offset = chunk * CHUNK + (place >> 3)
    wanted = lax.rem(me + offset, bricks) * CAP + (place & (CAP - 1))
    pick = jnp.where(wanted.astype(jnp.float32) == slot_row, 1.0, 0.0).astype(jnp.bfloat16)
    found = jnp.dot(pick, operand[...], preferred_element_type=jnp.float32)
    lower = (place & 7) < CAP
    high, low, weight = [
        jnp.where(
            lower,
            found[:, number * LANES : (number + 1) * LANES],
            found[:, (3 + number) * LANES : (4 + number) * LANES],
        )
        for number in range(3)
    ]
    packed = ((weight * WEIGHT_STEPS).astype(jnp.int32) << 15) + (high * LANES + low).astype(jnp.int32)
    base = pl.multiple_of(chunk * CHUNK, CHUNK)
    outgoing[pl.ds(base, CHUNK)] = packed.reshape(CHUNK, 8, LANES)

    def start(place_in, carry):
        step = base + place_in
        target = lax.rem(me + step, bricks)

        @pl.when(step > 0)
        def _():
            pltpu.make_async_remote_copy(
                src_ref=outgoing.at[step],
                dst_ref=arrived.at[step],
                send_sem=sent_sem,
                recv_sem=arrived_sem.at[step // GROUP],
                device_id=(target // along_y, lax.rem(target, along_y)),
                device_id_type=MESH,
            ).start()

        return carry

    lax.fori_loop(0, CHUNK, start, 0)


def one_hots(values, line):
    node = values[line : line + 1, :]
    high = (node >> 7) & 255
    low = node & 127
    weight = (node >> 15).astype(jnp.float32) * (1.0 / WEIGHT_STEPS)
    coarse = weight.astype(NARROW).astype(jnp.float32)
    rest = (weight - coarse) * REST_SCALE

    def wide(entry):
        return jnp.broadcast_to(entry.astype(jnp.float32), (16, LANES)).astype(jnp.bfloat16)

    high, low, coarse, rest = wide(high), wide(low), wide(coarse), wide(rest)
    counting = lax.broadcasted_iota(jnp.int32, (16, LANES), 0).astype(jnp.float32)
    one, zero = jnp.ones((16, LANES), jnp.bfloat16), jnp.zeros((16, LANES), jnp.bfloat16)
    rows, first, second = [], [], []
    for part in range(16):
        rows.append(jnp.where(high == (counting + 16 * part).astype(jnp.bfloat16), one, zero))
    for part in range(8):
        hit = low == (counting + 16 * part).astype(jnp.bfloat16)
        first.append(jnp.where(hit, coarse, zero))
        second.append(jnp.where(hit, rest, zero))
    return (
        jnp.concatenate(rows, 0).astype(NARROW),
        jnp.concatenate(first + second, 0).astype(NARROW),
    )


def raster_kernel(
    bricks, along_y, target_ref, count_ref, cell_ref, weight_ref, solid_ref,
    operand, outgoing, arrived, total, sent_sem, arrived_sem,
):
    me = lax.axis_index("gx") * along_y + lax.axis_index("gy")
    slot_row = brick_slots(me, bricks, target_ref, count_ref, cell_ref, weight_ref, operand)
    total[...] = jnp.zeros_like(total)

    def send(chunk, carry):
        send_chunk(
            me, bricks, along_y, chunk, slot_row, operand, outgoing, arrived, sent_sem, arrived_sem
        )
        return carry

    lax.fori_loop(0, bricks // CHUNK, send, 0)
    arrived[0] = outgoing[0]

    def add(group):
        left, right = [], []
        for member in range(GROUP):
            values = arrived[group * GROUP + member]
            for line in range(8):
                rows, columns = one_hots(values, line)
                left.append(rows)
                right.append(columns)
        total[...] += lax.dot_general(
            jnp.concatenate(left, 1),
            jnp.concatenate(right, 1),
            (((1,), (1,)), ((), ())),
            preferred_element_type=jnp.float32,
        )

    def landed(group, skip):
        whole = arrived.at[pl.ds(group * GROUP + skip, GROUP - skip)]
        pltpu.make_async_copy(whole, whole, arrived_sem.at[group]).wait()

    def later(group, carry):
        @pl.when(group == 0)
        def _():
            landed(0, 1)

        @pl.when(group > 0)
        def _():
            landed(group, 0)

        add(group)
        return carry

    lax.fori_loop(0, bricks // GROUP, later, 0)
    everything = outgoing.at[pl.ds(1, bricks - 1)]
    pltpu.make_async_copy(everything, everything, sent_sem).wait()
    density = total[:, :LANES] + total[:, LANES:] * (1.0 / REST_SCALE)
    solid_ref[...] = density / (1.0 + density)


def rasterize(block_brick, node_count, node_cell, node_weight, bricks, along_y):
    blocks, nodes = node_cell.shape
    return pl.pallas_call(
        functools.partial(raster_kernel, bricks, along_y),
        out_shape=jax.ShapeDtypeStruct((256, LANES), jnp.float32),
        in_specs=[pl.BlockSpec(memory_space=pltpu.VMEM)] * 4,
        out_specs=pl.BlockSpec(memory_space=pltpu.VMEM),
        scratch_shapes=[
            pltpu.VMEM((blocks, 6 * LANES), jnp.bfloat16),
            pltpu.VMEM((bricks, 8, LANES), jnp.int32),
            pltpu.VMEM((bricks, 8, LANES), jnp.int32),
            pltpu.VMEM((256, 2 * LANES), jnp.float32),
            pltpu.SemaphoreType.DMA,
            pltpu.SemaphoreType.DMA((bricks // GROUP,)),
        ],
        compiler_params=pltpu.CompilerParams(
            has_side_effects=True, vmem_limit_bytes=48 * 1024 * 1024
        ),
        name="rasterize",
    )(block_brick, node_count.reshape(1, blocks), node_cell, node_weight)


def on_device(populations, node_cell, node_weight, node_count, block_brick):
    along_y = lax.axis_size("gy")
    bricks = lax.axis_size("gx") * along_y
    solid = rasterize(block_brick, node_count, node_cell, node_weight, bricks, along_y)
    solid_frac = solid.reshape(32, 8, LANES).transpose(1, 0, 2).reshape(8, 32 * LANES)
    current = populations
    for repeat in range(STEPS):
        collided = collide(current, solid_frac)
        padded = extended(collided, (("gx", 1),), 1)
        padded = extended(padded, (("gy", 2),), NZ)
        current = stream_pull(padded)
    return (current, solid_frac)


def solution(mesh):
    return jax.shard_map(
        on_device,
        mesh=mesh,
        in_specs=(
            P(None, "gx", "gy"),
            P(("gx", "gy"), None),
            P(("gx", "gy"), None),
            P(("gx", "gy")),
            P(("gx", "gy"), None),
        ),
        out_specs=(P(None, "gx", "gy"), P("gx", "gy")),
        check_vma=False,
    )
```

```python
import functools

import jax
import jax.numpy as jnp
import numpy as np
from jax import lax
from jax.experimental import pallas as pl
from jax.experimental.pallas import tpu as pltpu
from jax.sharding import PartitionSpec as P

NZ = 64
STEPS = 3
CAP = 4
LANES = 128
GROUP = 8
CHUNK = 16
WEIGHT_STEPS = 1024.0
REST_SCALE = 64.0
MESH = pl.DeviceIdType.MESH
NARROW = jnp.float8_e4m3fn


lattice_velocities = (
    (0, 0, 0),
    (1, 0, 0),
    (-1, 0, 0),
    (0, 1, 0),
    (0, -1, 0),
    (0, 0, 1),
    (0, 0, -1),
    (1, 1, 0),
    (-1, -1, 0),
    (1, -1, 0),
    (-1, 1, 0),
    (1, 0, 1),
    (-1, 0, -1),
    (1, 0, -1),
    (-1, 0, 1),
    (0, 1, 1),
    (0, -1, -1),
    (0, 1, -1),
    (0, -1, 1),
)
opposite_of = (0, 2, 1, 4, 3, 6, 5, 8, 7, 10, 9, 12, 11, 14, 13, 16, 15, 18, 17)
lattice_weights = (1.0 / 3.0,) + (1.0 / 18.0,) * 6 + (1.0 / 36.0,) * 12


ROWS = 32
TOP = 8
TALL = 48
POPS = 19
RIGHT = (1, 7, 9, 11, 13)
LEFT = (2, 8, 10, 12, 14)
UP = (3, 7, 10, 15, 17)
DOWN = (4, 8, 9, 16, 18)


def place_of_lane():
    lane = lax.broadcasted_iota(jnp.int32, (8, LANES), 1)
    return lane < NZ, (lane & (NZ - 1)) == 0, (lane & (NZ - 1)) == NZ - 1


def pull(post, number, plane, tile):
    shift_x, shift_y, shift_z = lattice_velocities[number]
    even, z_first, z_last = place_of_lane()
    base = TOP + 8 * tile
    values = post[plane + 1 - shift_x, number, base : base + 8, :]
    turn = 0
    if shift_y == 1:
        values = jnp.where(even, values, post[plane + 1 - shift_x, number, base - 1 : base + 7, :])
        turn = NZ
    if shift_y == -1:
        values = jnp.where(even, post[plane + 1 - shift_x, number, base + 1 : base + 9, :], values)
        turn = NZ
    if shift_z == 0:
        return pltpu.roll(values, turn, 1) if turn else values
    near = pltpu.roll(values, (shift_z + turn) % LANES, 1)
    wrapped = pltpu.roll(values, (shift_z - shift_z * NZ + turn) % LANES, 1)
    return jnp.where(z_first if shift_z == 1 else z_last, wrapped, near)


def collide(f, solid):
    pairs = range(1, POPS, 2)
    sums = {i: f[i] + f[i + 1] for i in pairs}
    diffs = {i: f[i] - f[i + 1] for i in pairs}
    rho = f[0] + ((sums[1] + sums[3]) + (sums[5] + sums[7])) + (
        ((sums[9] + sums[11]) + (sums[13] + sums[15])) + sums[17]
    )
    jx = (diffs[1] + diffs[7]) + (diffs[9] + diffs[11]) + diffs[13]
    jy = (diffs[3] + diffs[7]) + (diffs[15] + diffs[17]) - diffs[9]
    jz = (diffs[5] + diffs[11]) + (diffs[15] - diffs[13]) - diffs[17]
    fluid = 1.0 - solid
    inverse = 1.0 / rho
    ux, uy, uz = jx * inverse, jy * inverse, jz * inverse
    jx, jy, jz = jx * fluid, jy * fluid, jz * fluid
    xx, yy, zz = jx * ux, jy * uy, jz * uz
    base = rho * fluid - 1.5 * (xx + yy + zz)
    hx, hy, hz = jx * (1.0 / 12.0), jy * (1.0 / 12.0), jz * (1.0 / 12.0)
    vx, vy, vz = ux * 1.5, uy * 1.5, uz * 1.5
    base_axis, base_diagonal = base * (1.0 / 18.0), base * (1.0 / 36.0)
    post = [base * (1.0 / 3.0) + solid * f[0]] + [None] * 18

    def put(i, even, odd):
        post[i] = (even + odd) + solid * f[i + 1]
        post[i + 1] = (even - odd) + solid * f[i]

    for i, square, h in ((1, xx, hx), (3, yy, hy), (5, zz, hz)):
        put(i, base_axis + 0.25 * square, 2.0 * h)
    for i, h, v in (
        (7, hx + hy, vx + vy),
        (9, hx - hy, vx - vy),
        (11, hx + hz, vx + vz),
        (13, hx - hz, vx - vz),
        (15, hy + hz, vy + vz),
        (17, hy - hz, vy - vz),
    ):
        put(i, base_diagonal + h * v, h)
    return post


def lattice(start, solid, result, result_out, posts, x_send, x_recv, y_send, y_recv, c_send, c_recv, sent, came, out_sem):
    here_x, here_y = lax.axis_index("gx"), lax.axis_index("gy")
    along_x, along_y = lax.axis_size("gx"), lax.axis_size("gy")
    ahead_x, behind_x = lax.rem(here_x + 1, along_x), lax.rem(here_x + along_x - 1, along_x)
    ahead_y, behind_y = lax.rem(here_y + 1, along_y), lax.rem(here_y + along_y - 1, along_y)
    partners = (
        (ahead_x, here_y),
        (behind_x, here_y),
        (here_x, ahead_y),
        (here_x, behind_y),
        (ahead_x, ahead_y),
        (behind_x, behind_y),
        (ahead_x, behind_y),
        (behind_x, ahead_y),
    )
    first, last = TOP, TOP + ROWS - 1

    def copy(step, way):
        if way < 2:
            source, landing = x_send.at[step, way], x_recv.at[step, way]
        elif way < 4:
            source, landing = y_send.at[step, way - 2], y_recv.at[step, way - 2]
        else:
            source, landing = c_send.at[step, way - 4], c_recv.at[step, way - 4]
        return pltpu.make_async_remote_copy(
            src_ref=source,
            dst_ref=landing,
            send_sem=sent.at[step, way],
            recv_sem=came.at[step, way],
            device_id=partners[way],
            device_id_type=MESH,
        )

    def send_x(step, post):
        for way, plane, group in ((0, 8, RIGHT), (1, 1, LEFT)):
            for place, number in enumerate(group):
                for half in range(2):
                    values = post[plane, number, first + 16 * half : first + 16 * half + 16, :]
                    at = place * ROWS + 16 * half
                    x_send[step, way, at : at + 16, :] = values.astype(jnp.bfloat16)
            copy(step, way).start()
        for way, number, plane, row in ((4, 7, 8, last - 7), (5, 8, 1, first), (6, 9, 8, first), (7, 10, 1, last - 7)):
            c_send[step, way - 4] = post[plane, number, row : row + 8, :]
            copy(step, way).start()

    def send_y(step, post):
        for way, row, group in ((2, last, UP), (3, first, DOWN)):
            for place, number in enumerate(group):
                for plane in range(8):
                    at = place * 8 + plane
                    y_send[step, way - 2, at : at + 1, :] = post[plane + 1, number, row : row + 1, :]
            copy(step, way).start()

    def receive(step, post):
        for way in range(8):
            copy(step, way).wait_recv()
        for way, plane, group in ((0, 0, RIGHT), (1, 9, LEFT)):
            for place, number in enumerate(group):
                for half in range(2):
                    at = place * ROWS + 16 * half
                    values = x_recv[step, way, at : at + 16, :]
                    post[plane, number, first + 16 * half : first + 16 * half + 16, :] = values.astype(jnp.float32)
        for way, row, group in ((2, first - 1, UP), (3, last + 1, DOWN)):
            for place, number in enumerate(group):
                for plane in range(8):
                    at = place * 8 + plane
                    post[plane + 1, number, row : row + 1, :] = y_recv[step, way - 2, at : at + 1, :]
        for way, number, plane, row, at in (
            (4, 7, 0, first - 1, 7),
            (5, 8, 9, last + 1, 0),
            (6, 9, 0, last + 1, 0),
            (7, 10, 9, first - 1, 7),
        ):
            post[plane, number, row : row + 1, :] = c_recv[step, way - 4, at : at + 1, :]

    def work(step, plane, tile):
        if step == 0:
            f = [start[i, pl.ds(64 * tile + plane, 8, stride=8), :] for i in range(POPS)]
        else:
            f = [pull(posts.at[(step - 1) % 2], i, plane, tile) for i in range(POPS)]
        post = collide(f, solid[plane, 8 * tile : 8 * tile + 8, :])
        base = TOP + 8 * tile
        for i in range(POPS):
            posts[step % 2, plane + 1, i, base : base + 8, :] = post[i]

    def inner(step):
        def planes(plane, carry):
            for tile in (1, 2):
                work(step, plane, tile)
            return carry

        lax.fori_loop(1, 7, planes, 0)

    def outer(step):
        post = posts.at[step % 2]

        def sides(side, carry):
            for tile in range(4):
                work(step, side * 7, tile)
            return carry

        lax.fori_loop(0, 2, sides, 0)
        send_x(step, post)

        def edges(plane, carry):
            for tile in (0, 3):
                work(step, plane, tile)
            return carry

        lax.fori_loop(1, 7, edges, 0)
        send_y(step, post)

    outer(0)
    inner(0)
    for step in range(1, STEPS):
        inner(step)
        receive(step - 1, posts.at[(step - 1) % 2])
        outer(step)
    post = posts.at[(STEPS - 1) % 2]

    def finish(number):
        def planes(plane, carry):
            for tile in range(4):
                result[number, pl.ds(64 * tile + plane, 8, stride=8), :] = pull(post, number, plane, tile)
            return carry

        lax.fori_loop(0, 8, planes, 0)
        pltpu.make_async_copy(result.at[number], result_out.at[number], out_sem.at[number]).start()

    for number in (0, 5, 6):
        finish(number)
    receive(STEPS - 1, post)
    for number in range(POPS):
        if number not in (0, 5, 6):
            finish(number)
    for step in range(STEPS):
        for way in range(8):
            copy(step, way).wait_send()
    for number in range(POPS):
        pltpu.make_async_copy(result.at[number], result_out.at[number], out_sem.at[number]).wait()


def lattice_scratch():
    return [
        pltpu.VMEM((2, 10, POPS, TALL, LANES), jnp.float32),
        pltpu.VMEM((STEPS, 2, 5 * ROWS, LANES), jnp.bfloat16),
        pltpu.VMEM((STEPS, 2, 5 * ROWS, LANES), jnp.bfloat16),
        pltpu.VMEM((STEPS, 2, 40, LANES), jnp.float32),
        pltpu.VMEM((STEPS, 2, 40, LANES), jnp.float32),
        pltpu.VMEM((STEPS, 4, 8, LANES), jnp.float32),
        pltpu.VMEM((STEPS, 4, 8, LANES), jnp.float32),
        pltpu.SemaphoreType.DMA((STEPS, 8)),
        pltpu.SemaphoreType.DMA((STEPS, 8)),
        pltpu.SemaphoreType.DMA((POPS,)),
    ]


def brick_slots(me, bricks, target_ref, count_ref, cell_ref, weight_ref, operand):
    blocks, nodes = cell_ref.shape
    row = lax.broadcasted_iota(jnp.int32, (blocks, blocks), 0)
    col = lax.broadcasted_iota(jnp.int32, (blocks, blocks), 1)
    target_col = target_ref[...]
    brick = lax.broadcasted_iota(jnp.int32, (blocks, bricks), 1)
    matches = jnp.where(brick == target_col, 1.0, 0.0)
    before = jnp.where(col < row, 1.0, 0.0).astype(jnp.bfloat16)
    earlier = jnp.dot(before, matches.astype(jnp.bfloat16), preferred_element_type=jnp.float32)
    rank = jnp.sum(earlier * matches, axis=1, keepdims=True)
    slot_col = target_col.astype(jnp.float32) * CAP + rank
    slot_row = jnp.sum(jnp.where(row == col, slot_col, 0.0), axis=0, keepdims=True)
    count_row = count_ref[...].astype(jnp.float32)
    count_col = jnp.sum(jnp.where(row == col, count_row, 0.0), axis=1, keepdims=True)
    node = lax.broadcasted_iota(jnp.int32, (blocks, nodes), 1).astype(jnp.float32)
    live = node < count_col
    cell = cell_ref[...]
    high = cell >> 7
    low = cell & 127
    weight = jnp.where(live, weight_ref[...].astype(jnp.float32), 0.0)
    for part in range(2):
        lanes = slice(part * LANES, (part + 1) * LANES)
        for number, values in enumerate((high.astype(jnp.float32), low.astype(jnp.float32), weight)):
            at = (part * 3 + number) * LANES
            operand[:, at : at + LANES] = values[:, lanes].astype(jnp.bfloat16)
    return slot_row


def send_chunk(me, bricks, along_y, chunk, slot_row, operand, outgoing, arrived, sent_sem, arrived_sem):
    rows = CHUNK * 8
    place = lax.broadcasted_iota(jnp.int32, (rows, 1), 0)
    offset = chunk * CHUNK + (place >> 3)
    wanted = lax.rem(me + offset, bricks) * CAP + (place & (CAP - 1))
    pick = jnp.where(wanted.astype(jnp.float32) == slot_row, 1.0, 0.0).astype(jnp.bfloat16)
    found = jnp.dot(pick, operand[...], preferred_element_type=jnp.float32)
    lower = (place & 7) < CAP
    high, low, weight = [
        jnp.where(
            lower,
            found[:, number * LANES : (number + 1) * LANES],
            found[:, (3 + number) * LANES : (4 + number) * LANES],
        )
        for number in range(3)
    ]
    packed = ((weight * WEIGHT_STEPS).astype(jnp.int32) << 15) + (high * LANES + low).astype(jnp.int32)
    base = pl.multiple_of(chunk * CHUNK, CHUNK)
    outgoing[pl.ds(base, CHUNK)] = packed.reshape(CHUNK, 8, LANES)

    def start(place_in, carry):
        step = base + place_in
        target = lax.rem(me + step, bricks)

        @pl.when(step > 0)
        def _():
            pltpu.make_async_remote_copy(
                src_ref=outgoing.at[step],
                dst_ref=arrived.at[step],
                send_sem=sent_sem,
                recv_sem=arrived_sem.at[step // GROUP],
                device_id=(target // along_y, lax.rem(target, along_y)),
                device_id_type=MESH,
            ).start()

        return carry

    lax.fori_loop(0, CHUNK, start, 0)


def one_hots(values, line):
    node = values[line : line + 1, :]
    high = (node >> 7) & 255
    low = node & 127
    weight = (node >> 15).astype(jnp.float32) * (1.0 / WEIGHT_STEPS)
    coarse = weight.astype(NARROW).astype(jnp.float32)
    rest = (weight - coarse) * REST_SCALE

    def wide(entry):
        return jnp.broadcast_to(entry.astype(jnp.float32), (16, LANES)).astype(jnp.bfloat16)

    high, low, coarse, rest = wide(high), wide(low), wide(coarse), wide(rest)
    counting = lax.broadcasted_iota(jnp.int32, (16, LANES), 0).astype(jnp.float32)
    one, zero = jnp.ones((16, LANES), jnp.bfloat16), jnp.zeros((16, LANES), jnp.bfloat16)
    rows, first, second = [], [], []
    for part in range(16):
        rows.append(jnp.where(high == (counting + 16 * part).astype(jnp.bfloat16), one, zero))
    for part in range(8):
        hit = low == (counting + 16 * part).astype(jnp.bfloat16)
        first.append(jnp.where(hit, coarse, zero))
        second.append(jnp.where(hit, rest, zero))
    return (
        jnp.concatenate(rows, 0).astype(NARROW),
        jnp.concatenate(first + second, 0).astype(NARROW),
    )


def program_kernel(
    bricks, along_y, target_ref, count_ref, cell_ref, weight_ref, start_hbm, solid_ref, result_hbm,
    operand, outgoing, arrived, total, start, solid, result, sent_sem, arrived_sem, start_sem, *lattice_refs,
):
    me = lax.axis_index("gx") * along_y + lax.axis_index("gy")
    loading = pltpu.make_async_copy(start_hbm, start, start_sem)
    loading.start()
    slot_row = brick_slots(me, bricks, target_ref, count_ref, cell_ref, weight_ref, operand)
    total[...] = jnp.zeros_like(total)

    def send(chunk, carry):
        send_chunk(
            me, bricks, along_y, chunk, slot_row, operand, outgoing, arrived, sent_sem, arrived_sem
        )
        return carry

    lax.fori_loop(0, bricks // CHUNK, send, 0)
    arrived[0] = outgoing[0]

    def add(group):
        left, right = [], []
        for member in range(GROUP):
            values = arrived[group * GROUP + member]
            for line in range(8):
                rows, columns = one_hots(values, line)
                left.append(rows)
                right.append(columns)
        total[...] += lax.dot_general(
            jnp.concatenate(left, 1),
            jnp.concatenate(right, 1),
            (((1,), (1,)), ((), ())),
            preferred_element_type=jnp.float32,
        )

    def landed(group, skip):
        whole = arrived.at[pl.ds(group * GROUP + skip, GROUP - skip)]
        pltpu.make_async_copy(whole, whole, arrived_sem.at[group]).wait()

    def later(group, carry):
        @pl.when(group == 0)
        def _():
            landed(0, 1)

        @pl.when(group > 0)
        def _():
            landed(group, 0)

        add(group)
        return carry

    lax.fori_loop(0, bricks // GROUP, later, 0)
    density = total[:, :LANES] + total[:, LANES:] * (1.0 / REST_SCALE)
    fraction = density / (1.0 + density)
    for plane in range(8):
        for tile in range(4):
            piece = fraction[plane * ROWS + 8 * tile : plane * ROWS + 8 * tile + 8, :]
            solid[plane, 8 * tile : 8 * tile + 8, :] = piece
            solid_ref[pl.ds(64 * tile + plane, 8, stride=8), :] = piece
    loading.wait()
    lattice(start, solid, result, result_hbm, *lattice_refs)
    everything = outgoing.at[pl.ds(1, bricks - 1)]
    pltpu.make_async_copy(everything, everything, sent_sem).wait()


def to_rows(values):
    lead = values.shape[:-2]
    return jnp.swapaxes(values.reshape(lead + (8, ROWS, LANES)), -3, -2).reshape(lead + (8 * ROWS, LANES))


def from_rows(values):
    lead = values.shape[:-2]
    return jnp.swapaxes(values.reshape(lead + (ROWS, 8, LANES)), -3, -2).reshape(lead + (8, ROWS * LANES))


def on_device(populations, node_cell, node_weight, node_count, block_brick):
    along_y = lax.axis_size("gy")
    bricks = lax.axis_size("gx") * along_y
    blocks, nodes = node_cell.shape
    vmem, anywhere = pl.BlockSpec(memory_space=pltpu.VMEM), pl.BlockSpec(memory_space=pl.ANY)
    solid, result = pl.pallas_call(
        functools.partial(program_kernel, bricks, along_y),
        out_shape=(
            jax.ShapeDtypeStruct((8 * ROWS, LANES), jnp.float32),
            jax.ShapeDtypeStruct((POPS, 8 * ROWS, LANES), jnp.float32),
        ),
        in_specs=[vmem, vmem, vmem, vmem, anywhere],
        out_specs=(vmem, anywhere),
        scratch_shapes=[
            pltpu.VMEM((blocks, 6 * LANES), jnp.bfloat16),
            pltpu.VMEM((bricks, 8, LANES), jnp.int32),
            pltpu.VMEM((bricks, 8, LANES), jnp.int32),
            pltpu.VMEM((8 * ROWS, 2 * LANES), jnp.float32),
            pltpu.VMEM((POPS, 8 * ROWS, LANES), jnp.float32),
            pltpu.VMEM((8, ROWS, LANES), jnp.float32),
            pltpu.VMEM((POPS, 8 * ROWS, LANES), jnp.float32),
            pltpu.SemaphoreType.DMA,
            pltpu.SemaphoreType.DMA((bricks // GROUP,)),
            pltpu.SemaphoreType.DMA,
        ]
        + lattice_scratch(),
        compiler_params=pltpu.CompilerParams(
            has_side_effects=True, vmem_limit_bytes=48 * 1024 * 1024
        ),
        name="permeability",
    )(block_brick, node_count.reshape(1, blocks), node_cell, node_weight, to_rows(populations))
    return (from_rows(result), from_rows(solid))


def solution(mesh):
    return jax.shard_map(
        on_device,
        mesh=mesh,
        in_specs=(
            P(None, "gx", "gy"),
            P(("gx", "gy"), None),
            P(("gx", "gy"), None),
            P(("gx", "gy")),
            P(("gx", "gy"), None),
        ),
        out_specs=(P(None, "gx", "gy"), P("gx", "gy")),
        check_vma=False,
    )
```

```python
import functools

import jax
import jax.numpy as jnp
import numpy as np
from jax import lax
from jax.experimental import pallas as pl
from jax.experimental.pallas import tpu as pltpu
from jax.sharding import PartitionSpec as P

NZ = 64
STEPS = 3
CAP = 4
LANES = 128
GROUP = 8
CHUNK = 16
WEIGHT_STEPS = 1024.0
REST_SCALE = 64.0
MESH = pl.DeviceIdType.MESH
NARROW = jnp.float8_e4m3fn


lattice_velocities = (
    (0, 0, 0),
    (1, 0, 0),
    (-1, 0, 0),
    (0, 1, 0),
    (0, -1, 0),
    (0, 0, 1),
    (0, 0, -1),
    (1, 1, 0),
    (-1, -1, 0),
    (1, -1, 0),
    (-1, 1, 0),
    (1, 0, 1),
    (-1, 0, -1),
    (1, 0, -1),
    (-1, 0, 1),
    (0, 1, 1),
    (0, -1, -1),
    (0, 1, -1),
    (0, -1, 1),
)
opposite_of = (0, 2, 1, 4, 3, 6, 5, 8, 7, 10, 9, 12, 11, 14, 13, 16, 15, 18, 17)
lattice_weights = (1.0 / 3.0,) + (1.0 / 18.0,) * 6 + (1.0 / 36.0,) * 12


ROWS = 32
TOP = 8
TALL = 48
POPS = 19
RIGHT = (1, 7, 9, 11, 13)
LEFT = (2, 8, 10, 12, 14)
UP = (3, 7, 10, 15, 17)
DOWN = (4, 8, 9, 16, 18)
UNSHIFTED = (0, 5, 6)


def place_of_lane():
    lane = lax.broadcasted_iota(jnp.int32, (8, LANES), 1)
    return lane < NZ, (lane & (NZ - 1)) == 0, (lane & (NZ - 1)) == NZ - 1


def pull(post, number, plane, tile):
    shift_x, shift_y, shift_z = lattice_velocities[number]
    even, z_first, z_last = place_of_lane()
    base = TOP + 8 * tile
    values = post[plane + 1 - shift_x, number, base : base + 8, :]
    turn = 0
    if shift_y == 1:
        values = jnp.where(even, values, post[plane + 1 - shift_x, number, base - 1 : base + 7, :])
        turn = NZ
    if shift_y == -1:
        values = jnp.where(even, post[plane + 1 - shift_x, number, base + 1 : base + 9, :], values)
        turn = NZ
    if shift_z == 0:
        return pltpu.roll(values, turn, 1) if turn else values
    near = pltpu.roll(values, (shift_z + turn) % LANES, 1)
    wrapped = pltpu.roll(values, (shift_z - shift_z * NZ + turn) % LANES, 1)
    return jnp.where(z_first if shift_z == 1 else z_last, wrapped, near)


def collide(f, solid):
    pairs = range(1, POPS, 2)
    sums = {i: f[i] + f[i + 1] for i in pairs}
    diffs = {i: f[i] - f[i + 1] for i in pairs}
    rho = f[0] + ((sums[1] + sums[3]) + (sums[5] + sums[7])) + (
        ((sums[9] + sums[11]) + (sums[13] + sums[15])) + sums[17]
    )
    jx = (diffs[1] + diffs[7]) + (diffs[9] + diffs[11]) + diffs[13]
    jy = (diffs[3] + diffs[7]) + (diffs[15] + diffs[17]) - diffs[9]
    jz = (diffs[5] + diffs[11]) + (diffs[15] - diffs[13]) - diffs[17]
    fluid = 1.0 - solid
    inverse = 1.0 / rho
    ux, uy, uz = jx * inverse, jy * inverse, jz * inverse
    jx, jy, jz = jx * fluid, jy * fluid, jz * fluid
    xx, yy, zz = jx * ux, jy * uy, jz * uz
    base = rho * fluid - 1.5 * (xx + yy + zz)
    hx, hy, hz = jx * (1.0 / 12.0), jy * (1.0 / 12.0), jz * (1.0 / 12.0)
    vx, vy, vz = ux * 1.5, uy * 1.5, uz * 1.5
    base_axis, base_diagonal = base * (1.0 / 18.0), base * (1.0 / 36.0)
    post = [base * (1.0 / 3.0) + solid * f[0]] + [None] * 18

    def put(i, even, odd):
        post[i] = (even + odd) + solid * f[i + 1]
        post[i + 1] = (even - odd) + solid * f[i]

    for i, square, h in ((1, xx, hx), (3, yy, hy), (5, zz, hz)):
        put(i, base_axis + 0.25 * square, 2.0 * h)
    for i, h, v in (
        (7, hx + hy, vx + vy),
        (9, hx - hy, vx - vy),
        (11, hx + hz, vx + vz),
        (13, hx - hz, vx - vz),
        (15, hy + hz, vy + vz),
        (17, hy - hz, vy - vz),
    ):
        put(i, base_diagonal + h * v, h)
    return post


def lattice(start, solid, result, posts, x_send, x_recv, y_send, y_recv, c_send, c_recv, sent, came):
    here_x, here_y = lax.axis_index("gx"), lax.axis_index("gy")
    along_x, along_y = lax.axis_size("gx"), lax.axis_size("gy")
    ahead_x, behind_x = lax.rem(here_x + 1, along_x), lax.rem(here_x + along_x - 1, along_x)
    ahead_y, behind_y = lax.rem(here_y + 1, along_y), lax.rem(here_y + along_y - 1, along_y)
    partners = (
        (ahead_x, here_y),
        (behind_x, here_y),
        (here_x, ahead_y),
        (here_x, behind_y),
        (ahead_x, ahead_y),
        (behind_x, behind_y),
        (ahead_x, behind_y),
        (behind_x, ahead_y),
    )
    first, last = TOP, TOP + ROWS - 1

    def copy(step, way):
        if way < 2:
            source, landing = x_send.at[step, way], x_recv.at[step, way]
        elif way < 4:
            source, landing = y_send.at[step, way - 2], y_recv.at[step, way - 2]
        else:
            source, landing = c_send.at[step, way - 4], c_recv.at[step, way - 4]
        return pltpu.make_async_remote_copy(
            src_ref=source,
            dst_ref=landing,
            send_sem=sent.at[step, way],
            recv_sem=came.at[step, way],
            device_id=partners[way],
            device_id_type=MESH,
        )

    def send_x(step, post):
        for way, plane, group in ((0, 8, RIGHT), (1, 1, LEFT)):
            for place, number in enumerate(group):
                for half in range(2):
                    values = post[plane, number, first + 16 * half : first + 16 * half + 16, :]
                    at = place * ROWS + 16 * half
                    x_send[step, way, at : at + 16, :] = values.astype(jnp.bfloat16)
            copy(step, way).start()
        for way, number, plane, row in ((4, 7, 8, last - 7), (5, 8, 1, first), (6, 9, 8, first), (7, 10, 1, last - 7)):
            c_send[step, way - 4] = post[plane, number, row : row + 8, :]
            copy(step, way).start()

    def send_y(step, post):
        for way, row, group in ((2, last, UP), (3, first, DOWN)):
            for place, number in enumerate(group):
                for plane in range(8):
                    at = place * 8 + plane
                    y_send[step, way - 2, at : at + 1, :] = post[plane + 1, number, row : row + 1, :]
            copy(step, way).start()

    def receive(step, post):
        for way in range(8):
            copy(step, way).wait_recv()
        for way, plane, group in ((0, 0, RIGHT), (1, 9, LEFT)):
            for place, number in enumerate(group):
                for half in range(2):
                    at = place * ROWS + 16 * half
                    values = x_recv[step, way, at : at + 16, :]
                    post[plane, number, first + 16 * half : first + 16 * half + 16, :] = values.astype(jnp.float32)
        for way, row, group in ((2, first - 1, UP), (3, last + 1, DOWN)):
            for place, number in enumerate(group):
                for plane in range(8):
                    at = place * 8 + plane
                    post[plane + 1, number, row : row + 1, :] = y_recv[step, way - 2, at : at + 1, :]
        for way, number, plane, row, at in (
            (4, 7, 0, first - 1, 7),
            (5, 8, 9, last + 1, 0),
            (6, 9, 0, last + 1, 0),
            (7, 10, 9, first - 1, 7),
        ):
            post[plane, number, row : row + 1, :] = c_recv[step, way - 4, at : at + 1, :]

    def work(step, plane, tile):
        if step == 0:
            f = [start[i, pl.ds(64 * tile + plane, 8, stride=8), :] for i in range(POPS)]
        else:
            f = [pull(posts.at[(step - 1) % 2], i, plane, tile) for i in range(POPS)]
        post = collide(f, solid[plane, 8 * tile : 8 * tile + 8, :])
        base = TOP + 8 * tile
        for i in range(POPS):
            posts[step % 2, plane + 1, i, base : base + 8, :] = post[i]

    def inner(step):
        def planes(plane, carry):
            for tile in (1, 2):
                work(step, plane, tile)
            return carry

        lax.fori_loop(1, 7, planes, 0)

    def outer(step):
        post = posts.at[step % 2]

        def sides(side, carry):
            for tile in range(4):
                work(step, side * 7, tile)
            return carry

        lax.fori_loop(0, 2, sides, 0)
        send_x(step, post)

        def edges(plane, carry):
            for tile in (0, 3):
                work(step, plane, tile)
            return carry

        lax.fori_loop(1, 7, edges, 0)
        send_y(step, post)

    outer(0)
    inner(0)
    for step in range(1, STEPS):
        inner(step)
        receive(step - 1, posts.at[(step - 1) % 2])
        outer(step)
    post = posts.at[(STEPS - 1) % 2]

    def finish(numbers):
        def planes(plane, carry):
            for number in numbers:
                for tile in range(4):
                    result[number, pl.ds(64 * tile + plane, 8, stride=8), :] = pull(post, number, plane, tile)
            return carry

        lax.fori_loop(0, 8, planes, 0)

    finish(UNSHIFTED)
    receive(STEPS - 1, post)
    finish([number for number in range(POPS) if number not in UNSHIFTED])
    for step in range(STEPS):
        for way in range(8):
            copy(step, way).wait_send()


def lattice_scratch():
    return [
        pltpu.VMEM((2, 10, POPS, TALL, LANES), jnp.float32),
        pltpu.VMEM((STEPS, 2, 5 * ROWS, LANES), jnp.bfloat16),
        pltpu.VMEM((STEPS, 2, 5 * ROWS, LANES), jnp.bfloat16),
        pltpu.VMEM((STEPS, 2, 40, LANES), jnp.float32),
        pltpu.VMEM((STEPS, 2, 40, LANES), jnp.float32),
        pltpu.VMEM((STEPS, 4, 8, LANES), jnp.float32),
        pltpu.VMEM((STEPS, 4, 8, LANES), jnp.float32),
        pltpu.SemaphoreType.DMA((STEPS, 8)),
        pltpu.SemaphoreType.DMA((STEPS, 8)),
    ]


def brick_slots(me, bricks, target_ref, count_ref, cell_ref, weight_ref, operand):
    blocks, nodes = cell_ref.shape
    row = lax.broadcasted_iota(jnp.int32, (blocks, blocks), 0)
    col = lax.broadcasted_iota(jnp.int32, (blocks, blocks), 1)
    target_row = target_ref[...].astype(jnp.float32)
    target_col = jnp.sum(jnp.where(row == col, target_row, 0.0), axis=1, keepdims=True)
    brick = lax.broadcasted_iota(jnp.int32, (blocks, bricks), 1)
    matches = jnp.where(brick.astype(jnp.float32) == target_col, 1.0, 0.0)
    before = jnp.where(col < row, 1.0, 0.0).astype(jnp.bfloat16)
    earlier = jnp.dot(before, matches.astype(jnp.bfloat16), preferred_element_type=jnp.float32)
    rank = jnp.sum(earlier * matches, axis=1, keepdims=True)
    slot_col = target_col * CAP + rank
    slot_row = jnp.sum(jnp.where(row == col, slot_col, 0.0), axis=0, keepdims=True)
    count_row = count_ref[...].astype(jnp.float32).reshape(1, blocks)
    count_col = jnp.sum(jnp.where(row == col, count_row, 0.0), axis=1, keepdims=True)
    node = lax.broadcasted_iota(jnp.int32, (blocks, nodes), 1).astype(jnp.float32)
    live = node < count_col
    cell = cell_ref[...]
    high = cell >> 7
    low = cell & 127
    weight = jnp.where(live, weight_ref[...].astype(jnp.float32), 0.0)
    for part in range(2):
        lanes = slice(part * LANES, (part + 1) * LANES)
        for number, values in enumerate((high.astype(jnp.float32), low.astype(jnp.float32), weight)):
            at = (part * 3 + number) * LANES
            operand[:, at : at + LANES] = values[:, lanes].astype(jnp.bfloat16)
    return slot_row


def send_chunk(me, bricks, along_y, chunk, slot_row, operand, outgoing, arrived, sent_sem, arrived_sem):
    rows = CHUNK * 8
    place = lax.broadcasted_iota(jnp.int32, (rows, 1), 0)
    offset = chunk * CHUNK + (place >> 3)
    wanted = lax.rem(me + offset, bricks) * CAP + (place & (CAP - 1))
    pick = jnp.where(wanted.astype(jnp.float32) == slot_row, 1.0, 0.0).astype(jnp.bfloat16)
    found = jnp.dot(pick, operand[...], preferred_element_type=jnp.float32)
    lower = (place & 7) < CAP
    high, low, weight = [
        jnp.where(
            lower,
            found[:, number * LANES : (number + 1) * LANES],
            found[:, (3 + number) * LANES : (4 + number) * LANES],
        )
        for number in range(3)
    ]
    packed = ((weight * WEIGHT_STEPS).astype(jnp.int32) << 15) + (high * LANES + low).astype(jnp.int32)
    base = pl.multiple_of(chunk * CHUNK, CHUNK)
    outgoing[pl.ds(base, CHUNK)] = packed.reshape(CHUNK, 8, LANES)

    def start(place_in, carry):
        step = base + place_in
        target = lax.rem(me + step, bricks)

        @pl.when(step > 0)
        def _():
            pltpu.make_async_remote_copy(
                src_ref=outgoing.at[step],
                dst_ref=arrived.at[step],
                send_sem=sent_sem,
                recv_sem=arrived_sem.at[step // GROUP],
                device_id=(target // along_y, lax.rem(target, along_y)),
                device_id_type=MESH,
            ).start()

        return carry

    lax.fori_loop(0, CHUNK, start, 0)


def one_hots(values, line):
    node = values[line : line + 1, :]
    high = (node >> 7) & 255
    low = node & 127
    weight = (node >> 15).astype(jnp.float32) * (1.0 / WEIGHT_STEPS)
    coarse = weight.astype(NARROW).astype(jnp.float32)
    rest = (weight - coarse) * REST_SCALE

    def wide(entry):
        return jnp.broadcast_to(entry.astype(jnp.float32), (16, LANES)).astype(jnp.bfloat16)

    high, low, coarse, rest = wide(high), wide(low), wide(coarse), wide(rest)
    counting = lax.broadcasted_iota(jnp.int32, (16, LANES), 0).astype(jnp.float32)
    one, zero = jnp.ones((16, LANES), jnp.bfloat16), jnp.zeros((16, LANES), jnp.bfloat16)
    rows, first, second = [], [], []
    for part in range(16):
        rows.append(jnp.where(high == (counting + 16 * part).astype(jnp.bfloat16), one, zero))
    for part in range(8):
        hit = low == (counting + 16 * part).astype(jnp.bfloat16)
        first.append(jnp.where(hit, coarse, zero))
        second.append(jnp.where(hit, rest, zero))
    return (
        jnp.concatenate(rows, 0).astype(NARROW),
        jnp.concatenate(first + second, 0).astype(NARROW),
    )


def program_kernel(
    bricks, along_y, target_hbm, count_hbm, cell_hbm, weight_hbm, start_hbm, solid_ref, result,
    target_ref, count_ref, cell_ref, weight_ref, start, operand, outgoing, arrived, total, solid,
    load_sem, sent_sem, arrived_sem, *lattice_refs,
):
    me = lax.axis_index("gx") * along_y + lax.axis_index("gy")
    sources = (target_hbm, count_hbm, cell_hbm, weight_hbm, start_hbm)
    landings = (target_ref, count_ref, cell_ref, weight_ref, start)
    loads = [
        pltpu.make_async_copy(source, landing, load_sem.at[number])
        for number, (source, landing) in enumerate(zip(sources, landings))
    ]
    for load in loads:
        load.start()
    barrier = pltpu.get_barrier_semaphore()

    def greet(step, carry):
        target = lax.rem(me + step, bricks)
        pl.semaphore_signal(
            barrier, inc=1, device_id=(target // along_y, lax.rem(target, along_y)), device_id_type=MESH
        )
        return carry

    lax.fori_loop(1, bricks, greet, 0)
    for load in loads[:4]:
        load.wait()
    slot_row = brick_slots(me, bricks, target_ref, count_ref, cell_ref, weight_ref, operand)
    pl.semaphore_wait(barrier, bricks - 1)
    total[...] = jnp.zeros_like(total)

    def send(chunk, carry):
        send_chunk(
            me, bricks, along_y, chunk, slot_row, operand, outgoing, arrived, sent_sem, arrived_sem
        )
        return carry

    lax.fori_loop(0, bricks // CHUNK, send, 0)
    arrived[0] = outgoing[0]

    def add(group):
        left, right = [], []
        for member in range(GROUP):
            values = arrived[group * GROUP + member]
            for line in range(8):
                rows, columns = one_hots(values, line)
                left.append(rows)
                right.append(columns)
        total[...] += lax.dot_general(
            jnp.concatenate(left, 1),
            jnp.concatenate(right, 1),
            (((1,), (1,)), ((), ())),
            preferred_element_type=jnp.float32,
        )

    def landed(group, skip):
        whole = arrived.at[pl.ds(group * GROUP + skip, GROUP - skip)]
        pltpu.make_async_copy(whole, whole, arrived_sem.at[group]).wait()

    def later(group, carry):
        @pl.when(group == 0)
        def _():
            landed(0, 1)

        @pl.when(group > 0)
        def _():
            landed(group, 0)

        add(group)
        return carry

    lax.fori_loop(0, bricks // GROUP, later, 0)
    density = total[:, :LANES] + total[:, LANES:] * (1.0 / REST_SCALE)
    fraction = density / (1.0 + density)
    for plane in range(8):
        for tile in range(4):
            piece = fraction[plane * ROWS + 8 * tile : plane * ROWS + 8 * tile + 8, :]
            solid[plane, 8 * tile : 8 * tile + 8, :] = piece
            solid_ref[pl.ds(64 * tile + plane, 8, stride=8), :] = piece
    loads[4].wait()
    lattice(start, solid, result, *lattice_refs)
    everything = outgoing.at[pl.ds(1, bricks - 1)]
    pltpu.make_async_copy(everything, everything, sent_sem).wait()


def to_rows(values):
    lead = values.shape[:-2]
    return jnp.swapaxes(values.reshape(lead + (8, ROWS, LANES)), -3, -2).reshape(lead + (8 * ROWS, LANES))


def from_rows(values):
    lead = values.shape[:-2]
    return jnp.swapaxes(values.reshape(lead + (ROWS, 8, LANES)), -3, -2).reshape(lead + (8, ROWS * LANES))


def on_device(populations, node_cell, node_weight, node_count, block_brick):
    along_y = lax.axis_size("gy")
    bricks = lax.axis_size("gx") * along_y
    blocks, nodes = node_cell.shape
    vmem, hbm = pl.BlockSpec(memory_space=pltpu.VMEM), pl.BlockSpec(memory_space=pltpu.HBM)
    solid, result = pl.pallas_call(
        functools.partial(program_kernel, bricks, along_y),
        out_shape=(
            jax.ShapeDtypeStruct((8 * ROWS, LANES), jnp.float32),
            jax.ShapeDtypeStruct((POPS, 8 * ROWS, LANES), jnp.float32),
        ),
        in_specs=[hbm] * 5,
        out_specs=(vmem, vmem),
        scratch_shapes=[
            pltpu.VMEM((1, blocks), jnp.int32),
            pltpu.VMEM((blocks,), jnp.int32),
            pltpu.VMEM((blocks, nodes), jnp.int32),
            pltpu.VMEM((blocks, nodes), jnp.bfloat16),
            pltpu.VMEM((POPS, 8 * ROWS, LANES), jnp.float32),
            pltpu.VMEM((blocks, 6 * LANES), jnp.bfloat16),
            pltpu.VMEM((bricks, 8, LANES), jnp.int32),
            pltpu.VMEM((bricks, 8, LANES), jnp.int32),
            pltpu.VMEM((8 * ROWS, 2 * LANES), jnp.float32),
            pltpu.VMEM((8, ROWS, LANES), jnp.float32),
            pltpu.SemaphoreType.DMA((5,)),
            pltpu.SemaphoreType.DMA,
            pltpu.SemaphoreType.DMA((bricks // GROUP,)),
        ]
        + lattice_scratch(),
        compiler_params=pltpu.CompilerParams(
            collective_id=0, has_side_effects=True, vmem_limit_bytes=48 * 1024 * 1024
        ),
        name="permeability",
    )(
        *(
            pltpu.with_memory_space_constraint(operand, pltpu.HBM)
            for operand in (
                block_brick.reshape(1, blocks), node_count, node_cell, node_weight, to_rows(populations)
            )
        )
    )
    return (from_rows(result), from_rows(solid))


def solution(mesh):
    return jax.shard_map(
        on_device,
        mesh=mesh,
        in_specs=(
            P(None, "gx", "gy"),
            P(("gx", "gy"), None),
            P(("gx", "gy"), None),
            P(("gx", "gy")),
            P(("gx", "gy"), None),
        ),
        out_specs=(P(None, "gx", "gy"), P("gx", "gy")),
        check_vma=False,
    )
```

```python
import functools

import jax
import jax.numpy as jnp
import numpy as np
from jax import lax
from jax.experimental import pallas as pl
from jax.experimental.pallas import tpu as pltpu
from jax.sharding import PartitionSpec as P

NZ = 64
STEPS = 3
CAP = 4
LANES = 128
GROUP = 16
CHUNK = 16
WEIGHT_STEPS = 1024.0
REST_SCALE = 64.0
MESH = pl.DeviceIdType.MESH
NARROW = jnp.float8_e4m3fn


lattice_velocities = (
    (0, 0, 0),
    (1, 0, 0),
    (-1, 0, 0),
    (0, 1, 0),
    (0, -1, 0),
    (0, 0, 1),
    (0, 0, -1),
    (1, 1, 0),
    (-1, -1, 0),
    (1, -1, 0),
    (-1, 1, 0),
    (1, 0, 1),
    (-1, 0, -1),
    (1, 0, -1),
    (-1, 0, 1),
    (0, 1, 1),
    (0, -1, -1),
    (0, 1, -1),
    (0, -1, 1),
)
opposite_of = (0, 2, 1, 4, 3, 6, 5, 8, 7, 10, 9, 12, 11, 14, 13, 16, 15, 18, 17)
lattice_weights = (1.0 / 3.0,) + (1.0 / 18.0,) * 6 + (1.0 / 36.0,) * 12


ROWS = 32
TOP = 8
TALL = 48
POPS = 19
RIGHT = (1, 7, 9, 11, 13)
LEFT = (2, 8, 10, 12, 14)
UP = (3, 7, 10, 15, 17)
DOWN = (4, 8, 9, 16, 18)
UNSHIFTED = (0, 5)


def pull(post, number, plane, tile):
    shift_x, shift_y, shift_z = lattice_velocities[number]
    even = lax.broadcasted_iota(jnp.int32, (8, LANES), 1) < NZ
    base = TOP + 8 * tile
    values = post[plane + 1 - shift_x, number, base : base + 8, :]
    turn = shift_z
    if shift_y == 1:
        values = jnp.where(even, values, post[plane + 1 - shift_x, number, base - 1 : base + 7, :])
        turn += NZ
    if shift_y == -1:
        values = jnp.where(even, post[plane + 1 - shift_x, number, base + 1 : base + 9, :], values)
        turn += NZ
    return pltpu.roll(values, turn % LANES, 1) if turn else values


def pull_pair(post, number, plane, tile):
    pair = [pull(post, number, plane, tile), pull(post, number + 1, plane, tile)]
    shift_z = lattice_velocities[number][2]
    if shift_z == 0:
        return pair
    z_place = lax.broadcasted_iota(jnp.int32, (8, LANES), 1) & (NZ - 1)
    edge, other = (0, NZ - 1) if shift_z == 1 else (NZ - 1, 0)
    turned = pltpu.roll(jnp.where(z_place == edge, pair[0], pair[1]), NZ, 1)
    return [jnp.where(z_place == edge, turned, pair[0]), jnp.where(z_place == other, turned, pair[1])]


def pull_all(post, plane, tile):
    values = [pull(post, 0, plane, tile)]
    for number in range(1, POPS, 2):
        values += pull_pair(post, number, plane, tile)
    return values


def collide(f, solid):
    pairs = range(1, POPS, 2)
    sums = {i: f[i] + f[i + 1] for i in pairs}
    diffs = {i: f[i] - f[i + 1] for i in pairs}
    rho = f[0] + ((sums[1] + sums[3]) + (sums[5] + sums[7])) + (
        ((sums[9] + sums[11]) + (sums[13] + sums[15])) + sums[17]
    )
    jx = (diffs[1] + diffs[7]) + (diffs[9] + diffs[11]) + diffs[13]
    jy = (diffs[3] + diffs[7]) + (diffs[15] + diffs[17]) - diffs[9]
    jz = (diffs[5] + diffs[11]) + (diffs[15] - diffs[13]) - diffs[17]
    fluid = 1.0 - solid
    inverse = 1.0 / rho
    ux, uy, uz = jx * inverse, jy * inverse, jz * inverse
    jx, jy, jz = jx * fluid, jy * fluid, jz * fluid
    xx, yy, zz = jx * ux, jy * uy, jz * uz
    base = rho * fluid - 1.5 * (xx + yy + zz)
    hx, hy, hz = jx * (1.0 / 12.0), jy * (1.0 / 12.0), jz * (1.0 / 12.0)
    vx, vy, vz = ux * 1.5, uy * 1.5, uz * 1.5
    base_axis, base_diagonal = base * (1.0 / 18.0), base * (1.0 / 36.0)
    post = [base * (1.0 / 3.0) + solid * f[0]] + [None] * 18

    def put(i, even, odd):
        post[i] = (even + odd) + solid * f[i + 1]
        post[i + 1] = (even - odd) + solid * f[i]

    for i, square, h in ((1, xx, hx), (3, yy, hy), (5, zz, hz)):
        put(i, base_axis + 0.25 * square, 2.0 * h)
    for i, h, v in (
        (7, hx + hy, vx + vy),
        (9, hx - hy, vx - vy),
        (11, hx + hz, vx + vz),
        (13, hx - hz, vx - vz),
        (15, hy + hz, vy + vz),
        (17, hy - hz, vy - vz),
    ):
        put(i, base_diagonal + h * v, h)
    return post


def lattice(start, solid, result, posts, x_send, x_recv, y_send, y_recv, c_send, c_recv, sent, came):
    here_x, here_y = lax.axis_index("gx"), lax.axis_index("gy")
    along_x, along_y = lax.axis_size("gx"), lax.axis_size("gy")
    ahead_x, behind_x = lax.rem(here_x + 1, along_x), lax.rem(here_x + along_x - 1, along_x)
    ahead_y, behind_y = lax.rem(here_y + 1, along_y), lax.rem(here_y + along_y - 1, along_y)
    partners = (
        (ahead_x, here_y),
        (behind_x, here_y),
        (here_x, ahead_y),
        (here_x, behind_y),
        (ahead_x, ahead_y),
        (behind_x, behind_y),
        (ahead_x, behind_y),
        (behind_x, ahead_y),
    )
    first, last = TOP, TOP + ROWS - 1

    def copy(step, way):
        if way < 2:
            source, landing = x_send.at[step, way], x_recv.at[step, way]
        elif way < 4:
            source, landing = y_send.at[step, way - 2], y_recv.at[step, way - 2]
        else:
            source, landing = c_send.at[step, way - 4], c_recv.at[step, way - 4]
        return pltpu.make_async_remote_copy(
            src_ref=source,
            dst_ref=landing,
            send_sem=sent.at[step, way],
            recv_sem=came.at[step, way],
            device_id=partners[way],
            device_id_type=MESH,
        )

    def send_x(step, post):
        for way, plane, group in ((0, 8, RIGHT), (1, 1, LEFT)):
            for place, number in enumerate(group):
                for half in range(2):
                    values = post[plane, number, first + 16 * half : first + 16 * half + 16, :]
                    at = place * ROWS + 16 * half
                    x_send[step, way, at : at + 16, :] = values.astype(jnp.bfloat16)
            copy(step, way).start()
        for way, number, plane, row in ((4, 7, 8, last - 7), (5, 8, 1, first), (6, 9, 8, first), (7, 10, 1, last - 7)):
            c_send[step, way - 4] = post[plane, number, row : row + 8, :]
            copy(step, way).start()

    def send_y(step, post):
        for way, row, group in ((2, last, UP), (3, first, DOWN)):
            for place, number in enumerate(group):
                for plane in range(8):
                    at = place * 8 + plane
                    y_send[step, way - 2, at : at + 1, :] = post[plane + 1, number, row : row + 1, :]
            copy(step, way).start()

    def receive(step, post):
        for way in range(8):
            copy(step, way).wait_recv()
        for way, plane, group in ((0, 0, RIGHT), (1, 9, LEFT)):
            for place, number in enumerate(group):
                for half in range(2):
                    at = place * ROWS + 16 * half
                    values = x_recv[step, way, at : at + 16, :]
                    post[plane, number, first + 16 * half : first + 16 * half + 16, :] = values.astype(jnp.float32)
        for way, row, group in ((2, first - 1, UP), (3, last + 1, DOWN)):
            for place, number in enumerate(group):
                for plane in range(8):
                    at = place * 8 + plane
                    post[plane + 1, number, row : row + 1, :] = y_recv[step, way - 2, at : at + 1, :]
        for way, number, plane, row, at in (
            (4, 7, 0, first - 1, 7),
            (5, 8, 9, last + 1, 0),
            (6, 9, 0, last + 1, 0),
            (7, 10, 9, first - 1, 7),
        ):
            post[plane, number, row : row + 1, :] = c_recv[step, way - 4, at : at + 1, :]

    def work(step, plane, tile):
        if step == 0:
            f = [start[i, pl.ds(64 * tile + plane, 8, stride=8), :] for i in range(POPS)]
        else:
            f = pull_all(posts.at[(step - 1) % 2], plane, tile)
        post = collide(f, solid[plane, 8 * tile : 8 * tile + 8, :])
        base = TOP + 8 * tile
        for i in range(POPS):
            posts[step % 2, plane + 1, i, base : base + 8, :] = post[i]

    def inner(step):
        def planes(plane, carry):
            for tile in (1, 2):
                work(step, plane, tile)
            return carry

        lax.fori_loop(1, 7, planes, 0)

    def outer(step):
        post = posts.at[step % 2]

        def sides(side, carry):
            for tile in range(4):
                work(step, side * 7, tile)
            return carry

        lax.fori_loop(0, 2, sides, 0)
        send_x(step, post)

        def edges(plane, carry):
            for tile in (0, 3):
                work(step, plane, tile)
            return carry

        lax.fori_loop(1, 7, edges, 0)
        send_y(step, post)

    outer(0)
    inner(0)
    for step in range(1, STEPS):
        inner(step)
        receive(step - 1, posts.at[(step - 1) % 2])
        outer(step)
    post = posts.at[(STEPS - 1) % 2]

    def finish(numbers):
        def planes(plane, carry):
            for tile in range(4):
                at = pl.ds(64 * tile + plane, 8, stride=8)
                for number in numbers:
                    if number == 0:
                        result[0, at, :] = pull(post, 0, plane, tile)
                    else:
                        result[number, at, :], result[number + 1, at, :] = pull_pair(post, number, plane, tile)
            return carry

        lax.fori_loop(0, 8, planes, 0)

    finish(UNSHIFTED)
    receive(STEPS - 1, post)
    finish([number for number in range(1, POPS, 2) if number not in UNSHIFTED])
    for step in range(STEPS):
        for way in range(8):
            copy(step, way).wait_send()


def lattice_scratch():
    return [
        pltpu.VMEM((2, 10, POPS, TALL, LANES), jnp.float32),
        pltpu.VMEM((STEPS, 2, 5 * ROWS, LANES), jnp.bfloat16),
        pltpu.VMEM((STEPS, 2, 5 * ROWS, LANES), jnp.bfloat16),
        pltpu.VMEM((STEPS, 2, 40, LANES), jnp.float32),
        pltpu.VMEM((STEPS, 2, 40, LANES), jnp.float32),
        pltpu.VMEM((STEPS, 4, 8, LANES), jnp.float32),
        pltpu.VMEM((STEPS, 4, 8, LANES), jnp.float32),
        pltpu.SemaphoreType.DMA((STEPS, 8)),
        pltpu.SemaphoreType.DMA((STEPS, 8)),
    ]


def brick_slots(me, bricks, target_ref, count_ref, cell_ref, weight_ref, operand):
    blocks, nodes = cell_ref.shape
    row = lax.broadcasted_iota(jnp.int32, (blocks, blocks), 0)
    col = lax.broadcasted_iota(jnp.int32, (blocks, blocks), 1)
    target_row = target_ref[...].astype(jnp.float32)
    target_col = jnp.sum(jnp.where(row == col, target_row, 0.0), axis=1, keepdims=True)
    brick = lax.broadcasted_iota(jnp.int32, (blocks, bricks), 1)
    matches = jnp.where(brick.astype(jnp.float32) == target_col, 1.0, 0.0)
    before = jnp.where(col < row, 1.0, 0.0).astype(jnp.bfloat16)
    earlier = jnp.dot(before, matches.astype(jnp.bfloat16), preferred_element_type=jnp.float32)
    rank = jnp.sum(earlier * matches, axis=1, keepdims=True)
    slot_col = target_col * CAP + rank
    slot_row = jnp.sum(jnp.where(row == col, slot_col, 0.0), axis=0, keepdims=True)
    count_row = count_ref[...].astype(jnp.float32).reshape(1, blocks)
    count_col = jnp.sum(jnp.where(row == col, count_row, 0.0), axis=1, keepdims=True)
    node = lax.broadcasted_iota(jnp.int32, (blocks, nodes), 1).astype(jnp.float32)
    live = node < count_col
    cell = cell_ref[...]
    high = cell >> 7
    low = cell & 127
    weight = jnp.where(live, weight_ref[...].astype(jnp.float32), 0.0)
    for part in range(2):
        lanes = slice(part * LANES, (part + 1) * LANES)
        for number, values in enumerate((high.astype(jnp.float32), low.astype(jnp.float32), weight)):
            at = (part * 3 + number) * LANES
            operand[:, at : at + LANES] = values[:, lanes].astype(jnp.bfloat16)
    return slot_row


def gather_slots(me, bricks, slot_row, operand, outgoing):
    rows = CHUNK * 8
    place = lax.broadcasted_iota(jnp.int32, (rows, 1), 0)

    def chunk_of(chunk, carry):
        offset = chunk * CHUNK + (place >> 3)
        wanted = lax.rem(me + offset, bricks) * CAP + (place & (CAP - 1))
        pick = jnp.where(wanted.astype(jnp.float32) == slot_row, 1.0, 0.0).astype(jnp.bfloat16)
        found = jnp.dot(pick, operand[...], preferred_element_type=jnp.float32)
        lower = (place & 7) < CAP
        high, low, weight = [
            jnp.where(
                lower,
                found[:, number * LANES : (number + 1) * LANES],
                found[:, (3 + number) * LANES : (4 + number) * LANES],
            )
            for number in range(3)
        ]
        packed = ((weight * WEIGHT_STEPS).astype(jnp.int32) << 15) + (high * LANES + low).astype(jnp.int32)
        base = pl.multiple_of(chunk * CHUNK, CHUNK)
        outgoing[pl.ds(base, CHUNK)] = packed.reshape(CHUNK, 8, LANES)
        return carry

    lax.fori_loop(0, bricks // CHUNK, chunk_of, 0)


def device_at(me, step, bricks, along_y):
    target = lax.rem(me + step, bricks)
    return lax.div(target, along_y), lax.rem(target, along_y)


def one_hots(values, line):
    node = values[line : line + 1, :]
    high = (node >> 7) & 255
    low = node & 127
    weight = (node >> 15).astype(jnp.float32) * (1.0 / WEIGHT_STEPS)
    coarse = weight.astype(NARROW).astype(jnp.float32)
    rest = (weight - coarse) * REST_SCALE

    def wide(entry):
        return jnp.broadcast_to(entry.astype(jnp.float32), (16, LANES)).astype(jnp.bfloat16)

    high, low, coarse, rest = wide(high), wide(low), wide(coarse), wide(rest)
    counting = lax.broadcasted_iota(jnp.int32, (16, LANES), 0).astype(jnp.float32)
    one, zero = jnp.ones((16, LANES), jnp.bfloat16), jnp.zeros((16, LANES), jnp.bfloat16)
    rows, first, second = [], [], []
    for part in range(16):
        rows.append(jnp.where(high == (counting + 16 * part).astype(jnp.bfloat16), one, zero))
    for part in range(8):
        hit = low == (counting + 16 * part).astype(jnp.bfloat16)
        first.append(jnp.where(hit, coarse, zero))
        second.append(jnp.where(hit, rest, zero))
    return (
        jnp.concatenate(rows, 0).astype(NARROW),
        jnp.concatenate(first + second, 0).astype(NARROW),
    )


def program_kernel(
    bricks, along_y, target_hbm, count_hbm, cell_hbm, weight_hbm, start_hbm, solid_ref, result,
    target_ref, count_ref, cell_ref, weight_ref, start, operand, outgoing, arrived, total, solid,
    load_sem, sent_sem, arrived_sem, *lattice_refs,
):
    me = lax.axis_index("gx") * along_y + lax.axis_index("gy")
    sources = (target_hbm, count_hbm, cell_hbm, weight_hbm, start_hbm)
    landings = (target_ref, count_ref, cell_ref, weight_ref, start)
    loads = [
        pltpu.make_async_copy(source, landing, load_sem.at[number])
        for number, (source, landing) in enumerate(zip(sources, landings))
    ]
    for load in loads:
        load.start()
    barrier = pltpu.get_barrier_semaphore()

    def greet(step, carry):
        pl.semaphore_signal(
            barrier, inc=1, device_id=device_at(me, step, bricks, along_y), device_id_type=MESH
        )
        return carry

    lax.fori_loop(1, bricks, greet, 0)
    for load in loads[:4]:
        load.wait()
    slot_row = brick_slots(me, bricks, target_ref, count_ref, cell_ref, weight_ref, operand)
    gather_slots(me, bricks, slot_row, operand, outgoing)
    total[...] = jnp.zeros_like(total)
    pl.semaphore_wait(barrier, bricks - 1)

    def send(step, carry):
        pltpu.make_async_remote_copy(
            src_ref=outgoing.at[step],
            dst_ref=arrived.at[step],
            send_sem=sent_sem,
            recv_sem=arrived_sem.at[lax.div(step, GROUP)],
            device_id=device_at(me, step, bricks, along_y),
            device_id_type=MESH,
        ).start()
        return carry

    lax.fori_loop(1, bricks, send, 0)
    arrived[0] = outgoing[0]

    def add(group):
        left, right = [], []
        for member in range(GROUP):
            values = arrived[group * GROUP + member]
            for line in range(8):
                rows, columns = one_hots(values, line)
                left.append(rows)
                right.append(columns)
        total[...] += lax.dot_general(
            jnp.concatenate(left, 1),
            jnp.concatenate(right, 1),
            (((1,), (1,)), ((), ())),
            preferred_element_type=jnp.float32,
        )

    def landed(group, skip):
        whole = arrived.at[pl.ds(group * GROUP + skip, GROUP - skip)]
        pltpu.make_async_copy(whole, whole, arrived_sem.at[group]).wait()

    def later(group, carry):
        @pl.when(group == 0)
        def _():
            landed(0, 1)

        @pl.when(group > 0)
        def _():
            landed(group, 0)

        add(group)
        return carry

    lax.fori_loop(0, bricks // GROUP, later, 0)
    density = total[:, :LANES] + total[:, LANES:] * (1.0 / REST_SCALE)
    fraction = density / (1.0 + density)
    for plane in range(8):
        for tile in range(4):
            piece = fraction[plane * ROWS + 8 * tile : plane * ROWS + 8 * tile + 8, :]
            solid[plane, 8 * tile : 8 * tile + 8, :] = piece
            solid_ref[pl.ds(64 * tile + plane, 8, stride=8), :] = piece
    loads[4].wait()
    lattice(start, solid, result, *lattice_refs)
    everything = outgoing.at[pl.ds(1, bricks - 1)]
    pltpu.make_async_copy(everything, everything, sent_sem).wait()


def to_rows(values):
    lead = values.shape[:-2]
    return jnp.swapaxes(values.reshape(lead + (8, ROWS, LANES)), -3, -2).reshape(lead + (8 * ROWS, LANES))


def from_rows(values):
    lead = values.shape[:-2]
    return jnp.swapaxes(values.reshape(lead + (ROWS, 8, LANES)), -3, -2).reshape(lead + (8, ROWS * LANES))


def on_device(populations, node_cell, node_weight, node_count, block_brick):
    along_y = lax.axis_size("gy")
    bricks = lax.axis_size("gx") * along_y
    blocks, nodes = node_cell.shape
    vmem, hbm = pl.BlockSpec(memory_space=pltpu.VMEM), pl.BlockSpec(memory_space=pltpu.HBM)
    solid, result = pl.pallas_call(
        functools.partial(program_kernel, bricks, along_y),
        out_shape=(
            jax.ShapeDtypeStruct((8 * ROWS, LANES), jnp.float32),
            jax.ShapeDtypeStruct((POPS, 8 * ROWS, LANES), jnp.float32),
        ),
        in_specs=[hbm] * 5,
        out_specs=(vmem, vmem),
        scratch_shapes=[
            pltpu.VMEM((1, blocks), jnp.int32),
            pltpu.VMEM((blocks,), jnp.int32),
            pltpu.VMEM((blocks, nodes), jnp.int32),
            pltpu.VMEM((blocks, nodes), jnp.bfloat16),
            pltpu.VMEM((POPS, 8 * ROWS, LANES), jnp.float32),
            pltpu.VMEM((blocks, 6 * LANES), jnp.bfloat16),
            pltpu.VMEM((bricks, 8, LANES), jnp.int32),
            pltpu.VMEM((bricks, 8, LANES), jnp.int32),
            pltpu.VMEM((8 * ROWS, 2 * LANES), jnp.float32),
            pltpu.VMEM((8, ROWS, LANES), jnp.float32),
            pltpu.SemaphoreType.DMA((5,)),
            pltpu.SemaphoreType.DMA,
            pltpu.SemaphoreType.DMA((bricks // GROUP,)),
        ]
        + lattice_scratch(),
        compiler_params=pltpu.CompilerParams(
            collective_id=0, has_side_effects=True, vmem_limit_bytes=48 * 1024 * 1024
        ),
        name="permeability",
    )(
        *(
            pltpu.with_memory_space_constraint(operand, pltpu.HBM)
            for operand in (
                block_brick.reshape(1, blocks), node_count, node_cell, node_weight, to_rows(populations)
            )
        )
    )
    return (from_rows(result), from_rows(solid))


def solution(mesh):
    return jax.shard_map(
        on_device,
        mesh=mesh,
        in_specs=(
            P(None, "gx", "gy"),
            P(("gx", "gy"), None),
            P(("gx", "gy"), None),
            P(("gx", "gy")),
            P(("gx", "gy"), None),
        ),
        out_specs=(P(None, "gx", "gy"), P("gx", "gy")),
        check_vma=False,
    )
```

```python
import functools

import jax
import jax.numpy as jnp
import numpy as np
from jax import lax
from jax.experimental import pallas as pl
from jax.experimental.pallas import tpu as pltpu
from jax.sharding import PartitionSpec as P

NZ = 64
STEPS = 3
CAP = 4
LANES = 128
GROUP = 16
CHUNK = 16
WEIGHT_STEPS = 1024.0
REST_SCALE = 64.0
MESH = pl.DeviceIdType.MESH
NARROW = jnp.float8_e4m3fn


lattice_velocities = (
    (0, 0, 0),
    (1, 0, 0),
    (-1, 0, 0),
    (0, 1, 0),
    (0, -1, 0),
    (0, 0, 1),
    (0, 0, -1),
    (1, 1, 0),
    (-1, -1, 0),
    (1, -1, 0),
    (-1, 1, 0),
    (1, 0, 1),
    (-1, 0, -1),
    (1, 0, -1),
    (-1, 0, 1),
    (0, 1, 1),
    (0, -1, -1),
    (0, 1, -1),
    (0, -1, 1),
)
opposite_of = (0, 2, 1, 4, 3, 6, 5, 8, 7, 10, 9, 12, 11, 14, 13, 16, 15, 18, 17)
lattice_weights = (1.0 / 3.0,) + (1.0 / 18.0,) * 6 + (1.0 / 36.0,) * 12


ROWS = 32
TOP = 8
TALL = 48
POPS = 19
WIDE = STEPS
PLANES = 8 + 2 * WIDE


def pull(read, number):
    shift_x, shift_y, shift_z = lattice_velocities[number]
    even = lax.broadcasted_iota(jnp.int32, (8, LANES), 1) < NZ
    values = read(number, shift_x, 0)
    turn = shift_z
    if shift_y == 1:
        values = jnp.where(even, values, read(number, shift_x, -1))
        turn += NZ
    if shift_y == -1:
        values = jnp.where(even, read(number, shift_x, 1), values)
        turn += NZ
    return pltpu.roll(values, turn % LANES, 1) if turn else values


def pull_pair(read, number):
    pair = [pull(read, number), pull(read, number + 1)]
    shift_z = lattice_velocities[number][2]
    if shift_z == 0:
        return pair
    z_place = lax.broadcasted_iota(jnp.int32, (8, LANES), 1) & (NZ - 1)
    edge, other = (0, NZ - 1) if shift_z == 1 else (NZ - 1, 0)
    turned = pltpu.roll(jnp.where(z_place == edge, pair[0], pair[1]), NZ, 1)
    return [jnp.where(z_place == edge, turned, pair[0]), jnp.where(z_place == other, turned, pair[1])]


def pull_all(read):
    values = [pull(read, 0)]
    for number in range(1, POPS, 2):
        values += pull_pair(read, number)
    return values


def collide(f, solid):
    pairs = range(1, POPS, 2)
    sums = {i: f[i] + f[i + 1] for i in pairs}
    diffs = {i: f[i] - f[i + 1] for i in pairs}
    rho = f[0] + ((sums[1] + sums[3]) + (sums[5] + sums[7])) + (
        ((sums[9] + sums[11]) + (sums[13] + sums[15])) + sums[17]
    )
    jx = (diffs[1] + diffs[7]) + (diffs[9] + diffs[11]) + diffs[13]
    jy = (diffs[3] + diffs[7]) + (diffs[15] + diffs[17]) - diffs[9]
    jz = (diffs[5] + diffs[11]) + (diffs[15] - diffs[13]) - diffs[17]
    fluid = 1.0 - solid
    inverse = 1.0 / rho
    ux, uy, uz = jx * inverse, jy * inverse, jz * inverse
    jx, jy, jz = jx * fluid, jy * fluid, jz * fluid
    xx, yy, zz = jx * ux, jy * uy, jz * uz
    base = rho * fluid - 1.5 * (xx + yy + zz)
    hx, hy, hz = jx * (1.0 / 12.0), jy * (1.0 / 12.0), jz * (1.0 / 12.0)
    vx, vy, vz = ux * 1.5, uy * 1.5, uz * 1.5
    base_axis, base_diagonal = base * (1.0 / 18.0), base * (1.0 / 36.0)
    post = [base * (1.0 / 3.0) + solid * f[0]] + [None] * 18

    def put(i, even, odd):
        post[i] = (even + odd) + solid * f[i + 1]
        post[i + 1] = (even - odd) + solid * f[i]

    for i, square, h in ((1, xx, hx), (3, yy, hy), (5, zz, hz)):
        put(i, base_axis + 0.25 * square, 2.0 * h)
    for i, h, v in (
        (7, hx + hy, vx + vy),
        (9, hx - hy, vx - vy),
        (11, hx + hz, vx + vz),
        (13, hx - hz, vx - vz),
        (15, hy + hz, vy + vz),
        (17, hy - hz, vy - vz),
    ):
        put(i, base_diagonal + h * v, h)
    return post


def partner_devices():
    here_x, here_y = lax.axis_index("gx"), lax.axis_index("gy")
    along_x, along_y = lax.axis_size("gx"), lax.axis_size("gy")
    ahead_x, behind_x = lax.rem(here_x + 1, along_x), lax.rem(here_x + along_x - 1, along_x)
    ahead_y, behind_y = lax.rem(here_y + 1, along_y), lax.rem(here_y + along_y - 1, along_y)
    return (
        (ahead_x, here_y),
        (behind_x, here_y),
        (here_x, ahead_y),
        (here_x, behind_y),
        (ahead_x, ahead_y),
        (behind_x, behind_y),
        (ahead_x, behind_y),
        (behind_x, ahead_y),
    )


SIDE = {2: 0, 4: 0, 7: 0, 3: 1, 5: 1, 6: 1}
HALO_WAYS = ((2, 4, 7), (3, 6, 5))


def start_copy(way, partners, x_send, x_recv, y_send, y_recv, sent, came):
    if way < 2:
        source, landing = x_send.at[way], x_recv.at[way]
    else:
        source, landing = y_send.at[SIDE[way]], y_recv.at[way - 2]
    return pltpu.make_async_remote_copy(
        src_ref=source, dst_ref=landing, send_sem=sent.at[way], recv_sem=came.at[way],
        device_id=partners[way], device_id_type=MESH,
    )


def solid_copy(way, partners, solid, y_send, y_recv, sent, came):
    if way == 0:
        source, landing = solid.at[pl.ds(8, WIDE)], solid.at[pl.ds(0, WIDE)]
    elif way == 1:
        source, landing = solid.at[pl.ds(WIDE, WIDE)], solid.at[pl.ds(8 + WIDE, WIDE)]
    else:
        source, landing = y_send.at[SIDE[way]], y_recv.at[way - 2]
    return pltpu.make_async_remote_copy(
        src_ref=source, dst_ref=landing, send_sem=sent.at[way], recv_sem=came.at[way],
        device_id=partners[way], device_id_type=MESH,
    )


def pack_start(start, x_send, y_send):
    def population(number, carry):
        for way, first in ((0, 8 - WIDE), (1, 0)):
            for plane in range(WIDE):
                for half in range(2):
                    rows = start[number, pl.ds(128 * half + first + plane, 16, stride=8), :]
                    x_send[way, plane, number, 16 * half : 16 * half + 16, :] = rows.astype(jnp.bfloat16)
        y_send[0, number] = start[number, 8 * ROWS - 16 : 8 * ROWS, :].astype(jnp.bfloat16)
        y_send[1, number] = start[number, 0:16, :].astype(jnp.bfloat16)
        return carry

    lax.fori_loop(0, POPS, population, 0)


def lattice(
    start, solid, result, partners, posts, fx_send, fx_recv, fy_send, fy_recv, f_sent, f_came,
    sy_send, sy_recv, s_sent, s_came, f_edge, s_edge,
):
    def start_halo(way):
        return start_copy(way, partners, fx_send, fx_recv, fy_send, fy_recv, f_sent, f_came)

    def solid_halo(way):
        return solid_copy(way, partners, solid, sy_send, sy_recv, s_sent, s_came)

    for way in range(8):
        solid_halo(way).start()

    def begin(plane, carry):
        for tile in range(4):
            f = [start[i, pl.ds(64 * tile + plane, 8, stride=8), :] for i in range(POPS)]
            post = collide(f, solid[plane + WIDE, 8 * tile : 8 * tile + 8, :])
            for i in range(POPS):
                posts[0, plane + WIDE, i, TOP + 8 * tile : TOP + 8 * tile + 8, :] = post[i]
        return carry

    def reader(source, plane, tile):
        base = TOP + 8 * tile
        return lambda number, shift_x, down: source[plane - shift_x, number, base + down : base + down + 8, :]

    def advance(step, plane, tile):
        f = pull_all(reader(posts.at[(step - 1) % 2], plane, tile))
        post = collide(f, solid[plane, 8 * tile : 8 * tile + 8, :])
        for i in range(POPS):
            posts[step % 2, plane, i, TOP + 8 * tile : TOP + 8 * tile + 8, :] = post[i]

    def planes_of(step, first, last, tiles):
        def body(plane, carry):
            for tile in tiles:
                advance(step, plane, tile)
            return carry

        lax.fori_loop(first, last, body, 0)

    def flat(step):
        return posts.at[step % 2].reshape(PLANES * POPS * TALL, LANES)

    def edge_rows(row, plane, number):
        return pl.ds((plane * POPS + number) * TALL + row, 8, stride=POPS * TALL)

    def edge(step, row, first):
        source, landing = flat(step - 1), flat(step)
        f = pull_all(lambda number, shift_x, down: source[edge_rows(row + down, first - shift_x, number), :])
        post = collide(f, s_edge[1 if row < TOP else 2, first : first + 8, :])
        for i in range(POPS):
            landing[edge_rows(row, first, i), :] = post[i]

    lax.fori_loop(0, 8, begin, 0)
    planes_of(1, 4, 10, (1, 2))

    for way in range(8):
        start_halo(way).wait_recv()

    def spread(number, carry):
        for side, ways in enumerate(HALO_WAYS):
            middle, below, above = [fy_recv[way - 2, number].astype(jnp.float32) for way in ways]
            for pair in range(2):
                f_edge[number, 2 * side + pair, WIDE : WIDE + 8, :] = middle[8 * pair : 8 * pair + 8]
                f_edge[number, 2 * side + pair, 0:WIDE, :] = below[8 * pair + 8 - WIDE : 8 * pair + 8]
                f_edge[number, 2 * side + pair, WIDE + 8 : PLANES, :] = above[8 * pair : 8 * pair + WIDE]
        return carry

    lax.fori_loop(0, POPS, spread, 0)
    for way in range(8):
        solid_halo(way).wait_recv()
    for side, ways in enumerate(HALO_WAYS):
        middle, below, above = [sy_recv[way - 2] for way in ways]
        for pair in range(2):
            s_edge[2 * side + pair, WIDE : WIDE + 8, :] = middle[8 * pair : 8 * pair + 8]
            s_edge[2 * side + pair, 0:WIDE, :] = below[8 * pair + 8 - WIDE : 8 * pair + 8]
            s_edge[2 * side + pair, WIDE + 8 : PLANES, :] = above[8 * pair : 8 * pair + WIDE]

    def begin_beside(plane, carry):
        for side in range(2):
            at = plane + side * (8 + WIDE)
            for half in range(2):
                f = [fx_recv[side, plane, i, 16 * half : 16 * half + 16, :].astype(jnp.float32) for i in range(POPS)]
                post = collide(f, solid[at, 16 * half : 16 * half + 16, :])
                for i in range(POPS):
                    posts[0, at, i, TOP + 16 * half : TOP + 16 * half + 16, :] = post[i]
        return carry

    lax.fori_loop(0, WIDE, begin_beside, 0)
    for place, row in enumerate((TOP - 2, TOP - 1, TOP + ROWS, TOP + ROWS + 1)):
        for first in (0, PLANES - 8):
            f = [f_edge[i, place, first : first + 8, :] for i in range(POPS)]
            post = collide(f, s_edge[place, first : first + 8, :])
            for i in range(POPS):
                flat(0)[edge_rows(row, first, i), :] = post[i]
    planes_of(1, 1, 4, range(4))
    planes_of(1, 10, 13, range(4))
    planes_of(1, 4, 10, (0, 3))
    for row in (TOP - 1, TOP + ROWS):
        for first in (1, 5):
            edge(1, row, first)
    planes_of(2, 2, 12, range(4))
    for row in (TOP - 1, TOP + ROWS):
        for first in (2, 4):
            edge(2, row, first)

    def finish(plane, carry):
        for tile in range(4):
            at = pl.ds(64 * tile + plane, 8, stride=8)
            read = reader(posts.at[0], plane + WIDE, tile)
            result[0, at, :] = pull(read, 0)
            for number in range(1, POPS, 2):
                result[number, at, :], result[number + 1, at, :] = pull_pair(read, number)
        return carry

    lax.fori_loop(0, 8, finish, 0)
    for way in range(8):
        start_halo(way).wait_send()
        solid_halo(way).wait_send()


def lattice_scratch():
    return [
        pltpu.VMEM((2, PLANES, POPS, TALL, LANES), jnp.float32),
        pltpu.VMEM((2, WIDE, POPS, ROWS, LANES), jnp.bfloat16),
        pltpu.VMEM((2, WIDE, POPS, ROWS, LANES), jnp.bfloat16),
        pltpu.VMEM((2, POPS, 16, LANES), jnp.bfloat16),
        pltpu.VMEM((6, POPS, 16, LANES), jnp.bfloat16),
        pltpu.SemaphoreType.DMA((8,)),
        pltpu.SemaphoreType.DMA((8,)),
        pltpu.VMEM((2, 16, LANES), jnp.float32),
        pltpu.VMEM((6, 16, LANES), jnp.float32),
        pltpu.SemaphoreType.DMA((8,)),
        pltpu.SemaphoreType.DMA((8,)),
        pltpu.VMEM((POPS, 4, 16, LANES), jnp.float32),
        pltpu.VMEM((4, 16, LANES), jnp.float32),
    ]


def brick_slots(me, bricks, target_ref, count_ref, cell_ref, weight_ref, operand):
    blocks, nodes = cell_ref.shape
    row = lax.broadcasted_iota(jnp.int32, (blocks, blocks), 0)
    col = lax.broadcasted_iota(jnp.int32, (blocks, blocks), 1)
    target_row = target_ref[...].astype(jnp.float32)
    target_col = jnp.sum(jnp.where(row == col, target_row, 0.0), axis=1, keepdims=True)
    brick = lax.broadcasted_iota(jnp.int32, (blocks, bricks), 1)
    matches = jnp.where(brick.astype(jnp.float32) == target_col, 1.0, 0.0)
    before = jnp.where(col < row, 1.0, 0.0).astype(jnp.bfloat16)
    earlier = jnp.dot(before, matches.astype(jnp.bfloat16), preferred_element_type=jnp.float32)
    rank = jnp.sum(earlier * matches, axis=1, keepdims=True)
    slot_col = target_col * CAP + rank
    slot_row = jnp.sum(jnp.where(row == col, slot_col, 0.0), axis=0, keepdims=True)
    count_row = count_ref[...].astype(jnp.float32).reshape(1, blocks)
    count_col = jnp.sum(jnp.where(row == col, count_row, 0.0), axis=1, keepdims=True)
    node = lax.broadcasted_iota(jnp.int32, (blocks, nodes), 1).astype(jnp.float32)
    live = node < count_col
    cell = cell_ref[...]
    high = cell >> 7
    low = cell & 127
    weight = jnp.where(live, weight_ref[...].astype(jnp.float32), 0.0)
    for part in range(2):
        lanes = slice(part * LANES, (part + 1) * LANES)
        for number, values in enumerate((high.astype(jnp.float32), low.astype(jnp.float32), weight)):
            at = (part * 3 + number) * LANES
            operand[:, at : at + LANES] = values[:, lanes].astype(jnp.bfloat16)
    return slot_row


def gather_slots(me, bricks, slot_row, operand, outgoing):
    rows = CHUNK * 8
    place = lax.broadcasted_iota(jnp.int32, (rows, 1), 0)

    def chunk_of(chunk, carry):
        offset = chunk * CHUNK + (place >> 3)
        wanted = lax.rem(me + offset, bricks) * CAP + (place & (CAP - 1))
        pick = jnp.where(wanted.astype(jnp.float32) == slot_row, 1.0, 0.0).astype(jnp.bfloat16)
        found = jnp.dot(pick, operand[...], preferred_element_type=jnp.float32)
        lower = (place & 7) < CAP
        high, low, weight = [
            jnp.where(
                lower,
                found[:, number * LANES : (number + 1) * LANES],
                found[:, (3 + number) * LANES : (4 + number) * LANES],
            )
            for number in range(3)
        ]
        packed = ((weight * WEIGHT_STEPS).astype(jnp.int32) << 15) + (high * LANES + low).astype(jnp.int32)
        base = pl.multiple_of(chunk * CHUNK, CHUNK)
        outgoing[pl.ds(base, CHUNK)] = packed.reshape(CHUNK, 8, LANES)
        return carry

    lax.fori_loop(0, bricks // CHUNK, chunk_of, 0)


def device_at(me, step, bricks, along_y):
    target = lax.rem(me + step, bricks)
    return lax.div(target, along_y), lax.rem(target, along_y)


def one_hots(values, line):
    node = values[line : line + 1, :]
    high = (node >> 7) & 255
    low = node & 127
    weight = (node >> 15).astype(jnp.float32) * (1.0 / WEIGHT_STEPS)
    coarse = weight.astype(NARROW).astype(jnp.float32)
    rest = (weight - coarse) * REST_SCALE

    def wide(entry):
        return jnp.broadcast_to(entry.astype(jnp.float32), (16, LANES)).astype(jnp.bfloat16)

    high, low, coarse, rest = wide(high), wide(low), wide(coarse), wide(rest)
    counting = lax.broadcasted_iota(jnp.int32, (16, LANES), 0).astype(jnp.float32)
    one, zero = jnp.ones((16, LANES), jnp.bfloat16), jnp.zeros((16, LANES), jnp.bfloat16)
    rows, first, second = [], [], []
    for part in range(16):
        rows.append(jnp.where(high == (counting + 16 * part).astype(jnp.bfloat16), one, zero))
    for part in range(8):
        hit = low == (counting + 16 * part).astype(jnp.bfloat16)
        first.append(jnp.where(hit, coarse, zero))
        second.append(jnp.where(hit, rest, zero))
    return (
        jnp.concatenate(rows, 0).astype(NARROW),
        jnp.concatenate(first + second, 0).astype(NARROW),
    )


def program_kernel(
    bricks, along_y, target_hbm, count_hbm, cell_hbm, weight_hbm, start_hbm, solid_ref, result,
    target_ref, count_ref, cell_ref, weight_ref, start, operand, outgoing, arrived, total, solid,
    load_sem, sent_sem, arrived_sem, *lattice_refs,
):
    posts, fx_send, fx_recv, fy_send, fy_recv, f_sent, f_came, sy_send = lattice_refs[:8]
    partners = partner_devices()
    me = lax.axis_index("gx") * along_y + lax.axis_index("gy")
    sources = (target_hbm, count_hbm, cell_hbm, weight_hbm, start_hbm)
    landings = (target_ref, count_ref, cell_ref, weight_ref, start)
    loads = [
        pltpu.make_async_copy(source, landing, load_sem.at[number])
        for number, (source, landing) in enumerate(zip(sources, landings))
    ]
    for load in loads:
        load.start()
    barrier = pltpu.get_barrier_semaphore()

    def greet(step, carry):
        pl.semaphore_signal(
            barrier, inc=1, device_id=device_at(me, step, bricks, along_y), device_id_type=MESH
        )
        return carry

    lax.fori_loop(1, bricks, greet, 0)
    for load in loads[:4]:
        load.wait()
    slot_row = brick_slots(me, bricks, target_ref, count_ref, cell_ref, weight_ref, operand)
    gather_slots(me, bricks, slot_row, operand, outgoing)
    loads[4].wait()
    pack_start(start, fx_send, fy_send)
    total[...] = jnp.zeros_like(total)
    pl.semaphore_wait(barrier, bricks - 1)

    def send(step, carry):
        pltpu.make_async_remote_copy(
            src_ref=outgoing.at[step],
            dst_ref=arrived.at[step],
            send_sem=sent_sem,
            recv_sem=arrived_sem.at[lax.div(step, GROUP)],
            device_id=device_at(me, step, bricks, along_y),
            device_id_type=MESH,
        ).start()
        return carry

    lax.fori_loop(1, bricks, send, 0)
    for way in range(8):
        start_copy(way, partners, fx_send, fx_recv, fy_send, fy_recv, f_sent, f_came).start()
    arrived[0] = outgoing[0]

    def add(group):
        left, right = [], []
        for member in range(GROUP):
            values = arrived[group * GROUP + member]
            for line in range(8):
                rows, columns = one_hots(values, line)
                left.append(rows)
                right.append(columns)
        total[...] += lax.dot_general(
            jnp.concatenate(left, 1),
            jnp.concatenate(right, 1),
            (((1,), (1,)), ((), ())),
            preferred_element_type=jnp.float32,
        )

    def landed(group, skip):
        whole = arrived.at[pl.ds(group * GROUP + skip, GROUP - skip)]
        pltpu.make_async_copy(whole, whole, arrived_sem.at[group]).wait()

    def later(group, carry):
        @pl.when(group == 0)
        def _():
            landed(0, 1)

        @pl.when(group > 0)
        def _():
            landed(group, 0)

        add(group)
        return carry

    lax.fori_loop(0, bricks // GROUP, later, 0)
    density = total[:, :LANES] + total[:, LANES:] * (1.0 / REST_SCALE)
    fraction = density / (1.0 + density)
    for plane in range(8):
        for tile in range(4):
            piece = fraction[plane * ROWS + 8 * tile : plane * ROWS + 8 * tile + 8, :]
            solid[plane + WIDE, 8 * tile : 8 * tile + 8, :] = piece
            solid_ref[pl.ds(64 * tile + plane, 8, stride=8), :] = piece
    sy_send[0] = solid_ref[8 * ROWS - 16 : 8 * ROWS, :]
    sy_send[1] = solid_ref[0:16, :]
    lattice(start, solid, result, partners, *lattice_refs)
    everything = outgoing.at[pl.ds(1, bricks - 1)]
    pltpu.make_async_copy(everything, everything, sent_sem).wait()


def to_rows(values):
    lead = values.shape[:-2]
    return jnp.swapaxes(values.reshape(lead + (8, ROWS, LANES)), -3, -2).reshape(lead + (8 * ROWS, LANES))


def from_rows(values):
    lead = values.shape[:-2]
    return jnp.swapaxes(values.reshape(lead + (ROWS, 8, LANES)), -3, -2).reshape(lead + (8, ROWS * LANES))


def on_device(populations, node_cell, node_weight, node_count, block_brick):
    along_y = lax.axis_size("gy")
    bricks = lax.axis_size("gx") * along_y
    blocks, nodes = node_cell.shape
    vmem, hbm = pl.BlockSpec(memory_space=pltpu.VMEM), pl.BlockSpec(memory_space=pltpu.HBM)
    solid, result = pl.pallas_call(
        functools.partial(program_kernel, bricks, along_y),
        out_shape=(
            jax.ShapeDtypeStruct((8 * ROWS, LANES), jnp.float32),
            jax.ShapeDtypeStruct((POPS, 8 * ROWS, LANES), jnp.float32),
        ),
        in_specs=[hbm] * 5,
        out_specs=(vmem, vmem),
        scratch_shapes=[
            pltpu.VMEM((1, blocks), jnp.int32),
            pltpu.VMEM((blocks,), jnp.int32),
            pltpu.VMEM((blocks, nodes), jnp.int32),
            pltpu.VMEM((blocks, nodes), jnp.bfloat16),
            pltpu.VMEM((POPS, 8 * ROWS, LANES), jnp.float32),
            pltpu.VMEM((blocks, 6 * LANES), jnp.bfloat16),
            pltpu.VMEM((bricks, 8, LANES), jnp.int32),
            pltpu.VMEM((bricks, 8, LANES), jnp.int32),
            pltpu.VMEM((8 * ROWS, 2 * LANES), jnp.float32),
            pltpu.VMEM((PLANES, ROWS, LANES), jnp.float32),
            pltpu.SemaphoreType.DMA((5,)),
            pltpu.SemaphoreType.DMA,
            pltpu.SemaphoreType.DMA((bricks // GROUP,)),
        ]
        + lattice_scratch(),
        compiler_params=pltpu.CompilerParams(
            collective_id=0, has_side_effects=True, vmem_limit_bytes=48 * 1024 * 1024
        ),
        name="permeability",
    )(
        *(
            pltpu.with_memory_space_constraint(operand, pltpu.HBM)
            for operand in (
                block_brick.reshape(1, blocks), node_count, node_cell, node_weight, to_rows(populations)
            )
        )
    )
    return (from_rows(result), from_rows(solid))


def solution(mesh):
    return jax.shard_map(
        on_device,
        mesh=mesh,
        in_specs=(
            P(None, "gx", "gy"),
            P(("gx", "gy"), None),
            P(("gx", "gy"), None),
            P(("gx", "gy")),
            P(("gx", "gy"), None),
        ),
        out_specs=(P(None, "gx", "gy"), P("gx", "gy")),
        check_vma=False,
    )
```

```python
import functools

import jax
import jax.numpy as jnp
import numpy as np
from jax import lax
from jax.experimental import pallas as pl
from jax.experimental.pallas import tpu as pltpu
from jax.sharding import PartitionSpec as P

NZ = 64
STEPS = 3
CAP = 4
LANES = 128
GROUP = 16
CHUNK = 16
WEIGHT_STEPS = 1024.0
REST_SCALE = 64.0
MESH = pl.DeviceIdType.MESH
NARROW = jnp.float8_e4m3fn


lattice_velocities = (
    (0, 0, 0),
    (1, 0, 0),
    (-1, 0, 0),
    (0, 1, 0),
    (0, -1, 0),
    (0, 0, 1),
    (0, 0, -1),
    (1, 1, 0),
    (-1, -1, 0),
    (1, -1, 0),
    (-1, 1, 0),
    (1, 0, 1),
    (-1, 0, -1),
    (1, 0, -1),
    (-1, 0, 1),
    (0, 1, 1),
    (0, -1, -1),
    (0, 1, -1),
    (0, -1, 1),
)
opposite_of = (0, 2, 1, 4, 3, 6, 5, 8, 7, 10, 9, 12, 11, 14, 13, 16, 15, 18, 17)
lattice_weights = (1.0 / 3.0,) + (1.0 / 18.0,) * 6 + (1.0 / 36.0,) * 12


ROWS = 32
TOP = 8
TALL = 48
POPS = 19
RIGHT = (1, 7, 9, 11, 13)
LEFT = (2, 8, 10, 12, 14)
WIDE = STEPS
NEAR = WIDE - 1
PLANES = 8 + 2 * WIDE


def pull(read, number):
    shift_x, shift_y, shift_z = lattice_velocities[number]
    lane = lax.broadcasted_iota(jnp.int32, (8, LANES), 1)
    even, z_place = lane < NZ, lane & (NZ - 1)
    values = read(number, shift_x, 0)
    turn = 0
    if shift_y == 1:
        values = jnp.where(even, values, read(number, shift_x, -1))
        turn = NZ
    if shift_y == -1:
        values = jnp.where(even, read(number, shift_x, 1), values)
        turn = NZ
    if shift_z == 0:
        return pltpu.roll(values, turn, 1) if turn else values
    near = pltpu.roll(values, (shift_z + turn) % LANES, 1)
    wrapped = pltpu.roll(values, (shift_z + NZ + turn) % LANES, 1)
    return jnp.where(z_place == (0 if shift_z == 1 else NZ - 1), wrapped, near)


def pull_pair(read, number):
    return [pull(read, number), pull(read, number + 1)]


def pull_all(read):
    return [pull(read, number) for number in range(POPS)]


def collide(f, solid):
    pairs = range(1, POPS, 2)
    sums = {i: f[i] + f[i + 1] for i in pairs}
    diffs = {i: f[i] - f[i + 1] for i in pairs}
    rho = f[0] + ((sums[1] + sums[3]) + (sums[5] + sums[7])) + (
        ((sums[9] + sums[11]) + (sums[13] + sums[15])) + sums[17]
    )
    jx = (diffs[1] + diffs[7]) + (diffs[9] + diffs[11]) + diffs[13]
    jy = (diffs[3] + diffs[7]) + (diffs[15] + diffs[17]) - diffs[9]
    jz = (diffs[5] + diffs[11]) + (diffs[15] - diffs[13]) - diffs[17]
    fluid = 1.0 - solid
    inverse = 1.0 / rho
    ux, uy, uz = jx * inverse, jy * inverse, jz * inverse
    jx, jy, jz = jx * fluid, jy * fluid, jz * fluid
    xx, yy, zz = jx * ux, jy * uy, jz * uz
    base = rho * fluid - 1.5 * (xx + yy + zz)
    hx, hy, hz = jx * (1.0 / 12.0), jy * (1.0 / 12.0), jz * (1.0 / 12.0)
    vx, vy, vz = ux * 1.5, uy * 1.5, uz * 1.5
    base_axis, base_diagonal = base * (1.0 / 18.0), base * (1.0 / 36.0)
    post = [base * (1.0 / 3.0) + solid * f[0]] + [None] * 18

    def put(i, even, odd):
        post[i] = (even + odd) + solid * f[i + 1]
        post[i + 1] = (even - odd) + solid * f[i]

    for i, square, h in ((1, xx, hx), (3, yy, hy), (5, zz, hz)):
        put(i, base_axis + 0.25 * square, 2.0 * h)
    for i, h, v in (
        (7, hx + hy, vx + vy),
        (9, hx - hy, vx - vy),
        (11, hx + hz, vx + vz),
        (13, hx - hz, vx - vz),
        (15, hy + hz, vy + vz),
        (17, hy - hz, vy - vz),
    ):
        put(i, base_diagonal + h * v, h)
    return post


def partner_devices():
    here_x, here_y = lax.axis_index("gx"), lax.axis_index("gy")
    along_x, along_y = lax.axis_size("gx"), lax.axis_size("gy")
    ahead_x, behind_x = lax.rem(here_x + 1, along_x), lax.rem(here_x + along_x - 1, along_x)
    ahead_y, behind_y = lax.rem(here_y + 1, along_y), lax.rem(here_y + along_y - 1, along_y)
    return (
        (ahead_x, here_y),
        (behind_x, here_y),
        (here_x, ahead_y),
        (here_x, behind_y),
        (ahead_x, ahead_y),
        (behind_x, behind_y),
        (ahead_x, behind_y),
        (behind_x, ahead_y),
    )


SIDE = {2: 0, 4: 0, 7: 0, 3: 1, 5: 1, 6: 1}
HALO_WAYS = ((2, 4, 7), (3, 6, 5))


def start_copy(way, partners, x_send, x_recv, y_send, y_recv, sent, came):
    if way < 2:
        source, landing = x_send.at[way], x_recv.at[way]
    else:
        source, landing = y_send.at[SIDE[way]], y_recv.at[way - 2]
    return pltpu.make_async_remote_copy(
        src_ref=source, dst_ref=landing, send_sem=sent.at[way], recv_sem=came.at[way],
        device_id=partners[way], device_id_type=MESH,
    )


def solid_copy(way, partners, solid, y_send, y_recv, sent, came):
    if way == 0:
        source, landing = solid.at[pl.ds(9, NEAR)], solid.at[pl.ds(1, NEAR)]
    elif way == 1:
        source, landing = solid.at[pl.ds(WIDE, NEAR)], solid.at[pl.ds(8 + WIDE, NEAR)]
    else:
        source, landing = y_send.at[SIDE[way]], y_recv.at[way - 2]
    return pltpu.make_async_remote_copy(
        src_ref=source, dst_ref=landing, send_sem=sent.at[way], recv_sem=came.at[way],
        device_id=partners[way], device_id_type=MESH,
    )


def pack_start(start, x_send, y_send):
    def population(number, carry):
        for way, first in ((0, 8 - NEAR), (1, 0)):
            for plane in range(NEAR):
                for half in range(2):
                    rows = start[number, pl.ds(128 * half + first + plane, 16, stride=8), :]
                    x_send[way, plane, number, 16 * half : 16 * half + 16, :] = rows.astype(jnp.bfloat16)
        y_send[0, number] = start[number, 8 * ROWS - 16 : 8 * ROWS, :].astype(jnp.bfloat16)
        y_send[1, number] = start[number, 0:16, :].astype(jnp.bfloat16)
        return carry

    lax.fori_loop(0, POPS, population, 0)


def lattice(
    start, solid, result, partners, even_posts, odd_posts, even_stage, odd_stage, fx_send, fx_recv, fy_send, fy_recv, f_sent, f_came,
    sy_send, sy_recv, s_sent, s_came, f_edge, s_edge, far_send, far_recv, far_sent, far_came,
):
    posts = (even_posts, odd_posts)

    def start_halo(way):
        return start_copy(way, partners, fx_send, fx_recv, fy_send, fy_recv, f_sent, f_came)

    def solid_halo(way):
        return solid_copy(way, partners, solid, sy_send, sy_recv, s_sent, s_came)

    for way in range(8):
        solid_halo(way).start()

    def begin(plane, carry):
        for tile in range(4):
            f = [start[i, pl.ds(64 * tile + plane, 8, stride=8), :] for i in range(POPS)]
            post = collide(f, solid[plane + WIDE, 8 * tile : 8 * tile + 8, :])
            for i in range(POPS):
                posts[0][plane + WIDE, i, TOP + 8 * tile : TOP + 8 * tile + 8, :] = post[i]
        return carry

    def reader(source, plane, tile):
        base = TOP + 8 * tile
        return lambda number, shift_x, down: source[plane - shift_x, number, base + down : base + down + 8, :]

    def fetch(step, plane, tiles, stage):
        for tile in tiles:
            f = pull_all(reader(posts[(step - 1) % 2], plane, tile))
            for i in range(POPS):
                stage[tile, i] = f[i]

    def settle(step, plane, tiles, stage):
        for tile in tiles:
            post = collide([stage[tile, i] for i in range(POPS)], solid[plane, 8 * tile : 8 * tile + 8, :])
            for i in range(POPS):
                posts[step % 2][plane, i, TOP + 8 * tile : TOP + 8 * tile + 8, :] = post[i]

    def planes_of(step, first, last, tiles):
        def body(pair, carry):
            plane = first + 2 * pair
            fetch(step, plane + 1, tiles, odd_stage)
            settle(step, plane, tiles, even_stage)
            fetch(step, jnp.minimum(plane + 2, last - 1), tiles, even_stage)
            settle(step, plane + 1, tiles, odd_stage)
            return carry

        fetch(step, first, tiles, even_stage)
        lax.fori_loop(0, (last - first) // 2, body, 0)
        if (last - first) % 2:
            settle(step, last - 1, tiles, even_stage)

    def flat(step):
        return posts[step % 2].reshape(PLANES * POPS * TALL, LANES)

    def edge_rows(row, plane, number):
        return pl.ds((plane * POPS + number) * TALL + row, 8, stride=POPS * TALL)

    def edge(step, row, first):
        source, landing = flat(step - 1), flat(step)
        f = pull_all(lambda number, shift_x, down: source[edge_rows(row + down, first - shift_x, number), :])
        post = collide(f, s_edge[1 if row < TOP else 2, first : first + 8, :])
        for i in range(POPS):
            landing[edge_rows(row, first, i), :] = post[i]

    def far_copy(way):
        return pltpu.make_async_remote_copy(
            src_ref=far_send.at[way], dst_ref=far_recv.at[way], send_sem=far_sent.at[way], recv_sem=far_came.at[way],
            device_id=partners[way], device_id_type=MESH,
        )

    lax.fori_loop(0, 2, lambda side, carry: begin(8 - WIDE - side * (8 - 2 * WIDE + 1), carry), 0)
    for way, plane, group in ((0, 8, RIGHT), (1, 2 * WIDE - 1, LEFT)):
        for place, number in enumerate(group):
            for half in range(2):
                rows = posts[0][plane, number, TOP + 16 * half : TOP + 16 * half + 16, :]
                at = place * ROWS + 16 * half
                far_send[way, at : at + 16, :] = rows.astype(jnp.bfloat16)
        far_copy(way).start()
    lax.fori_loop(0, 6, lambda place, carry: begin(place + lax.div(place, 2), carry), 0)
    planes_of(1, 4, 10, (1, 2))

    for way in range(8):
        start_halo(way).wait_recv()

    def spread(number, carry):
        for side, ways in enumerate(HALO_WAYS):
            middle, below, above = [fy_recv[way - 2, number].astype(jnp.float32) for way in ways]
            for pair in range(2):
                f_edge[number, 2 * side + pair, WIDE : WIDE + 8, :] = middle[8 * pair : 8 * pair + 8]
                f_edge[number, 2 * side + pair, 0:WIDE, :] = below[8 * pair + 8 - WIDE : 8 * pair + 8]
                f_edge[number, 2 * side + pair, WIDE + 8 : PLANES, :] = above[8 * pair : 8 * pair + WIDE]
        return carry

    lax.fori_loop(0, POPS, spread, 0)
    for way in range(8):
        solid_halo(way).wait_recv()
    for side, ways in enumerate(HALO_WAYS):
        middle, below, above = [sy_recv[way - 2] for way in ways]
        for pair in range(2):
            s_edge[2 * side + pair, WIDE : WIDE + 8, :] = middle[8 * pair : 8 * pair + 8]
            s_edge[2 * side + pair, 0:WIDE, :] = below[8 * pair + 8 - WIDE : 8 * pair + 8]
            s_edge[2 * side + pair, WIDE + 8 : PLANES, :] = above[8 * pair : 8 * pair + WIDE]

    def begin_beside(plane, carry):
        for side in range(2):
            at = plane + (1 if side == 0 else 8 + WIDE)
            for half in range(2):
                f = [fx_recv[side, plane, i, 16 * half : 16 * half + 16, :].astype(jnp.float32) for i in range(POPS)]
                post = collide(f, solid[at, 16 * half : 16 * half + 16, :])
                for i in range(POPS):
                    posts[0][at, i, TOP + 16 * half : TOP + 16 * half + 16, :] = post[i]
        return carry

    lax.fori_loop(0, NEAR, begin_beside, 0)
    for way, plane, group in ((0, 0, RIGHT), (1, PLANES - 1, LEFT)):
        far_copy(way).wait_recv()
        for place, number in enumerate(group):
            for half in range(2):
                at = place * ROWS + 16 * half
                rows = far_recv[way, at : at + 16, :]
                posts[0][plane, number, TOP + 16 * half : TOP + 16 * half + 16, :] = rows.astype(jnp.float32)
    for place, row in enumerate((TOP - 2, TOP - 1, TOP + ROWS, TOP + ROWS + 1)):
        for first in (0, PLANES - 8):
            f = [f_edge[i, place, first : first + 8, :] for i in range(POPS)]
            post = collide(f, s_edge[place, first : first + 8, :])
            for i in range(POPS):
                flat(0)[edge_rows(row, first, i), :] = post[i]
    planes_of(1, 1, 4, range(4))
    planes_of(1, 10, 13, range(4))
    planes_of(1, 4, 10, (0, 3))
    for row in (TOP - 1, TOP + ROWS):
        for first in (1, 5):
            edge(1, row, first)
    planes_of(2, 2, 12, range(4))
    for row in (TOP - 1, TOP + ROWS):
        for first in (2, 4):
            edge(2, row, first)

    def finish(plane, carry):
        for tile in range(4):
            at = pl.ds(64 * tile + plane, 8, stride=8)
            read = reader(posts[0], plane + WIDE, tile)
            result[0, at, :] = pull(read, 0)
            for number in range(1, POPS, 2):
                result[number, at, :], result[number + 1, at, :] = pull_pair(read, number)
        return carry

    lax.fori_loop(0, 8, finish, 0)
    for way in range(8):
        start_halo(way).wait_send()
        solid_halo(way).wait_send()
    for way in range(2):
        far_copy(way).wait_send()


def lattice_scratch():
    return [
        pltpu.VMEM((PLANES, POPS, TALL, LANES), jnp.float32),
        pltpu.VMEM((PLANES, POPS, TALL, LANES), jnp.float32),
        pltpu.VMEM((4, POPS, 8, LANES), jnp.float32),
        pltpu.VMEM((4, POPS, 8, LANES), jnp.float32),
        pltpu.VMEM((2, NEAR, POPS, ROWS, LANES), jnp.bfloat16),
        pltpu.VMEM((2, NEAR, POPS, ROWS, LANES), jnp.bfloat16),
        pltpu.VMEM((2, POPS, 16, LANES), jnp.bfloat16),
        pltpu.VMEM((6, POPS, 16, LANES), jnp.bfloat16),
        pltpu.SemaphoreType.DMA((8,)),
        pltpu.SemaphoreType.DMA((8,)),
        pltpu.VMEM((2, 16, LANES), jnp.float32),
        pltpu.VMEM((6, 16, LANES), jnp.float32),
        pltpu.SemaphoreType.DMA((8,)),
        pltpu.SemaphoreType.DMA((8,)),
        pltpu.VMEM((POPS, 4, 16, LANES), jnp.float32),
        pltpu.VMEM((4, 16, LANES), jnp.float32),
        pltpu.VMEM((2, 5 * ROWS, LANES), jnp.bfloat16),
        pltpu.VMEM((2, 5 * ROWS, LANES), jnp.bfloat16),
        pltpu.SemaphoreType.DMA((2,)),
        pltpu.SemaphoreType.DMA((2,)),
    ]


def brick_slots(me, bricks, target_ref, count_ref, cell_ref, weight_ref, operand):
    blocks, nodes = cell_ref.shape
    row = lax.broadcasted_iota(jnp.int32, (blocks, blocks), 0)
    col = lax.broadcasted_iota(jnp.int32, (blocks, blocks), 1)
    target_row = target_ref[...].astype(jnp.float32)
    target_col = jnp.sum(jnp.where(row == col, target_row, 0.0), axis=1, keepdims=True)
    brick = lax.broadcasted_iota(jnp.int32, (blocks, bricks), 1)
    matches = jnp.where(brick.astype(jnp.float32) == target_col, 1.0, 0.0)
    before = jnp.where(col < row, 1.0, 0.0).astype(jnp.bfloat16)
    earlier = jnp.dot(before, matches.astype(jnp.bfloat16), preferred_element_type=jnp.float32)
    rank = jnp.sum(earlier * matches, axis=1, keepdims=True)
    slot_col = target_col * CAP + rank
    slot_row = jnp.sum(jnp.where(row == col, slot_col, 0.0), axis=0, keepdims=True)
    count_row = count_ref[...].astype(jnp.float32).reshape(1, blocks)
    count_col = jnp.sum(jnp.where(row == col, count_row, 0.0), axis=1, keepdims=True)
    node = lax.broadcasted_iota(jnp.int32, (blocks, nodes), 1).astype(jnp.float32)
    live = node < count_col
    cell = cell_ref[...]
    high = cell >> 7
    low = cell & 127
    weight = jnp.where(live, weight_ref[...].astype(jnp.float32), 0.0)
    for part in range(2):
        lanes = slice(part * LANES, (part + 1) * LANES)
        for number, values in enumerate((high.astype(jnp.float32), low.astype(jnp.float32), weight)):
            at = (part * 3 + number) * LANES
            operand[:, at : at + LANES] = values[:, lanes].astype(jnp.bfloat16)
    return slot_row


def gather_slots(me, bricks, slot_row, operand, outgoing):
    rows = CHUNK * 8
    place = lax.broadcasted_iota(jnp.int32, (rows, 1), 0)

    def chunk_of(chunk, carry):
        offset = chunk * CHUNK + (place >> 3)
        wanted = lax.rem(me + offset, bricks) * CAP + (place & (CAP - 1))
        pick = jnp.where(wanted.astype(jnp.float32) == slot_row, 1.0, 0.0).astype(jnp.bfloat16)
        found = jnp.dot(pick, operand[...], preferred_element_type=jnp.float32)
        lower = (place & 7) < CAP
        high, low, weight = [
            jnp.where(
                lower,
                found[:, number * LANES : (number + 1) * LANES],
                found[:, (3 + number) * LANES : (4 + number) * LANES],
            )
            for number in range(3)
        ]
        packed = ((weight * WEIGHT_STEPS).astype(jnp.int32) << 15) + (high * LANES + low).astype(jnp.int32)
        base = pl.multiple_of(chunk * CHUNK, CHUNK)
        outgoing[pl.ds(base, CHUNK)] = packed.reshape(CHUNK, 8, LANES)
        return carry

    lax.fori_loop(0, bricks // CHUNK, chunk_of, 0)


def device_at(me, step, bricks, along_y):
    target = lax.rem(me + step, bricks)
    return lax.div(target, along_y), lax.rem(target, along_y)


def one_hots(values, line):
    node = values[line : line + 1, :]
    high = (node >> 7) & 255
    low = node & 127
    weight = (node >> 15).astype(jnp.float32) * (1.0 / WEIGHT_STEPS)
    coarse = weight.astype(NARROW).astype(jnp.float32)
    rest = (weight - coarse) * REST_SCALE

    def wide(entry):
        return jnp.broadcast_to(entry.astype(jnp.float32), (16, LANES)).astype(jnp.bfloat16)

    high, low, coarse, rest = wide(high), wide(low), wide(coarse), wide(rest)
    counting = lax.broadcasted_iota(jnp.int32, (16, LANES), 0).astype(jnp.float32)
    one, zero = jnp.ones((16, LANES), jnp.bfloat16), jnp.zeros((16, LANES), jnp.bfloat16)
    rows, first, second = [], [], []
    for part in range(16):
        rows.append(jnp.where(high == (counting + 16 * part).astype(jnp.bfloat16), one, zero))
    for part in range(8):
        hit = low == (counting + 16 * part).astype(jnp.bfloat16)
        first.append(jnp.where(hit, coarse, zero))
        second.append(jnp.where(hit, rest, zero))
    return (
        jnp.concatenate(rows, 0).astype(NARROW),
        jnp.concatenate(first + second, 0).astype(NARROW),
    )


def program_kernel(
    bricks, along_y, target_hbm, count_hbm, cell_hbm, weight_hbm, start_hbm, solid_ref, result,
    target_ref, count_ref, cell_ref, weight_ref, start, operand, outgoing, arrived, total, solid,
    load_sem, sent_sem, arrived_sem, *lattice_refs,
):
    fx_send, fx_recv, fy_send, fy_recv, f_sent, f_came, sy_send = lattice_refs[4:11]
    partners = partner_devices()
    me = lax.axis_index("gx") * along_y + lax.axis_index("gy")
    sources = (target_hbm, count_hbm, cell_hbm, weight_hbm, start_hbm)
    landings = (target_ref, count_ref, cell_ref, weight_ref, start)
    loads = [
        pltpu.make_async_copy(source, landing, load_sem.at[number])
        for number, (source, landing) in enumerate(zip(sources, landings))
    ]
    for load in loads:
        load.start()
    barrier = pltpu.get_barrier_semaphore()

    def greet(step, carry):
        pl.semaphore_signal(
            barrier, inc=1, device_id=device_at(me, step, bricks, along_y), device_id_type=MESH
        )
        return carry

    lax.fori_loop(1, bricks, greet, 0)
    for load in loads[:4]:
        load.wait()
    slot_row = brick_slots(me, bricks, target_ref, count_ref, cell_ref, weight_ref, operand)
    gather_slots(me, bricks, slot_row, operand, outgoing)
    loads[4].wait()
    pack_start(start, fx_send, fy_send)
    total[...] = jnp.zeros_like(total)
    pl.semaphore_wait(barrier, bricks - 1)

    def send(step, carry):
        pltpu.make_async_remote_copy(
            src_ref=outgoing.at[step],
            dst_ref=arrived.at[step],
            send_sem=sent_sem,
            recv_sem=arrived_sem.at[lax.div(step, GROUP)],
            device_id=device_at(me, step, bricks, along_y),
            device_id_type=MESH,
        ).start()
        return carry

    lax.fori_loop(1, bricks, send, 0)
    arrived[0] = outgoing[0]

    def add(group):
        left, right = [], []
        for member in range(GROUP):
            values = arrived[group * GROUP + member]
            for line in range(8):
                rows, columns = one_hots(values, line)
                left.append(rows)
                right.append(columns)
        total[...] += lax.dot_general(
            jnp.concatenate(left, 1),
            jnp.concatenate(right, 1),
            (((1,), (1,)), ((), ())),
            preferred_element_type=jnp.float32,
        )

    def landed(group, skip):
        whole = arrived.at[pl.ds(group * GROUP + skip, GROUP - skip)]
        pltpu.make_async_copy(whole, whole, arrived_sem.at[group]).wait()

    def later(group, carry):
        @pl.when(group == 0)
        def _():
            landed(0, 1)

        @pl.when(group > 0)
        def _():
            landed(group, 0)

        @pl.when(group == 0)
        def _():
            for way in range(8):
                start_copy(way, partners, fx_send, fx_recv, fy_send, fy_recv, f_sent, f_came).start()

        add(group)
        return carry

    lax.fori_loop(0, bricks // GROUP, later, 0)
    density = total[:, :LANES] + total[:, LANES:] * (1.0 / REST_SCALE)
    fraction = density / (1.0 + density)
    for plane in range(8):
        for tile in range(4):
            piece = fraction[plane * ROWS + 8 * tile : plane * ROWS + 8 * tile + 8, :]
            solid[plane + WIDE, 8 * tile : 8 * tile + 8, :] = piece
            solid_ref[pl.ds(64 * tile + plane, 8, stride=8), :] = piece
    sy_send[0] = solid_ref[8 * ROWS - 16 : 8 * ROWS, :]
    sy_send[1] = solid_ref[0:16, :]
    lattice(start, solid, result, partners, *lattice_refs)
    everything = outgoing.at[pl.ds(1, bricks - 1)]
    pltpu.make_async_copy(everything, everything, sent_sem).wait()


def to_rows(values):
    lead = values.shape[:-2]
    return jnp.swapaxes(values.reshape(lead + (8, ROWS, LANES)), -3, -2).reshape(lead + (8 * ROWS, LANES))


def from_rows(values):
    lead = values.shape[:-2]
    return jnp.swapaxes(values.reshape(lead + (ROWS, 8, LANES)), -3, -2).reshape(lead + (8, ROWS * LANES))


def on_device(populations, node_cell, node_weight, node_count, block_brick):
    along_y = lax.axis_size("gy")
    bricks = lax.axis_size("gx") * along_y
    blocks, nodes = node_cell.shape
    vmem, hbm = pl.BlockSpec(memory_space=pltpu.VMEM), pl.BlockSpec(memory_space=pltpu.HBM)
    solid, result = pl.pallas_call(
        functools.partial(program_kernel, bricks, along_y),
        out_shape=(
            jax.ShapeDtypeStruct((8 * ROWS, LANES), jnp.float32),
            jax.ShapeDtypeStruct((POPS, 8 * ROWS, LANES), jnp.float32),
        ),
        in_specs=[hbm] * 5,
        out_specs=(vmem, vmem),
        scratch_shapes=[
            pltpu.VMEM((1, blocks), jnp.int32),
            pltpu.VMEM((blocks,), jnp.int32),
            pltpu.VMEM((blocks, nodes), jnp.int32),
            pltpu.VMEM((blocks, nodes), jnp.bfloat16),
            pltpu.VMEM((POPS, 8 * ROWS, LANES), jnp.float32),
            pltpu.VMEM((blocks, 6 * LANES), jnp.bfloat16),
            pltpu.VMEM((bricks, 8, LANES), jnp.int32),
            pltpu.VMEM((bricks, 8, LANES), jnp.int32),
            pltpu.VMEM((8 * ROWS, 2 * LANES), jnp.float32),
            pltpu.VMEM((PLANES, ROWS, LANES), jnp.float32),
            pltpu.SemaphoreType.DMA((5,)),
            pltpu.SemaphoreType.DMA,
            pltpu.SemaphoreType.DMA((bricks // GROUP,)),
        ]
        + lattice_scratch(),
        compiler_params=pltpu.CompilerParams(
            collective_id=0, has_side_effects=True, vmem_limit_bytes=48 * 1024 * 1024
        ),
        name="permeability",
    )(
        *(
            pltpu.with_memory_space_constraint(operand, pltpu.HBM)
            for operand in (
                block_brick.reshape(1, blocks), node_count, node_cell, node_weight, to_rows(populations)
            )
        )
    )
    return (from_rows(result), from_rows(solid))


def solution(mesh):
    return jax.shard_map(
        on_device,
        mesh=mesh,
        in_specs=(
            P(None, "gx", "gy"),
            P(("gx", "gy"), None),
            P(("gx", "gy"), None),
            P(("gx", "gy")),
            P(("gx", "gy"), None),
        ),
        out_specs=(P(None, "gx", "gy"), P("gx", "gy")),
        check_vma=False,
    )
```

```python
import functools

import jax
import jax.numpy as jnp
import numpy as np
from jax import lax
from jax.experimental import pallas as pl
from jax.experimental.pallas import tpu as pltpu
from jax.sharding import PartitionSpec as P

NZ = 64
STEPS = 3
CAP = 4
LANES = 128
GROUP = 16
CHUNK = 16
WEIGHT_STEPS = 1024.0
REST_SCALE = 64.0
MESH = pl.DeviceIdType.MESH
NARROW = jnp.float8_e4m3fn


lattice_velocities = (
    (0, 0, 0),
    (1, 0, 0),
    (-1, 0, 0),
    (0, 1, 0),
    (0, -1, 0),
    (0, 0, 1),
    (0, 0, -1),
    (1, 1, 0),
    (-1, -1, 0),
    (1, -1, 0),
    (-1, 1, 0),
    (1, 0, 1),
    (-1, 0, -1),
    (1, 0, -1),
    (-1, 0, 1),
    (0, 1, 1),
    (0, -1, -1),
    (0, 1, -1),
    (0, -1, 1),
)
opposite_of = (0, 2, 1, 4, 3, 6, 5, 8, 7, 10, 9, 12, 11, 14, 13, 16, 15, 18, 17)
lattice_weights = (1.0 / 3.0,) + (1.0 / 18.0,) * 6 + (1.0 / 36.0,) * 12


ROWS = 32
TOP = 8
TALL = 48
POPS = 19
RIGHT = (1, 7, 9, 11, 13)
LEFT = (2, 8, 10, 12, 14)
WIDE = STEPS
NEAR = WIDE - 1
PLANES = 8 + 2 * WIDE


def pull(read, number):
    shift_x, shift_y, shift_z = lattice_velocities[number]
    lane = lax.broadcasted_iota(jnp.int32, (8, LANES), 1)
    even, z_place = lane < NZ, lane & (NZ - 1)
    values = read(number, shift_x, 0)
    turn = 0
    if shift_y == 1:
        values = jnp.where(even, values, read(number, shift_x, -1))
        turn = NZ
    if shift_y == -1:
        values = jnp.where(even, read(number, shift_x, 1), values)
        turn = NZ
    if shift_z == 0:
        return pltpu.roll(values, turn, 1) if turn else values
    near = pltpu.roll(values, (shift_z + turn) % LANES, 1)
    wrapped = pltpu.roll(values, (shift_z + NZ + turn) % LANES, 1)
    return jnp.where(z_place == (0 if shift_z == 1 else NZ - 1), wrapped, near)


def pull_pair(read, number):
    return [pull(read, number), pull(read, number + 1)]


def pull_all(read):
    return [pull(read, number) for number in range(POPS)]


def collide(f, solid):
    pairs = range(1, POPS, 2)
    sums = {i: f[i] + f[i + 1] for i in pairs}
    diffs = {i: f[i] - f[i + 1] for i in pairs}
    rho = f[0] + ((sums[1] + sums[3]) + (sums[5] + sums[7])) + (
        ((sums[9] + sums[11]) + (sums[13] + sums[15])) + sums[17]
    )
    jx = (diffs[1] + diffs[7]) + (diffs[9] + diffs[11]) + diffs[13]
    jy = (diffs[3] + diffs[7]) + (diffs[15] + diffs[17]) - diffs[9]
    jz = (diffs[5] + diffs[11]) + (diffs[15] - diffs[13]) - diffs[17]
    fluid = 1.0 - solid
    inverse = 1.0 / rho
    ux, uy, uz = jx * inverse, jy * inverse, jz * inverse
    jx, jy, jz = jx * fluid, jy * fluid, jz * fluid
    xx, yy, zz = jx * ux, jy * uy, jz * uz
    base = rho * fluid - 1.5 * (xx + yy + zz)
    hx, hy, hz = jx * (1.0 / 12.0), jy * (1.0 / 12.0), jz * (1.0 / 12.0)
    vx, vy, vz = ux * 1.5, uy * 1.5, uz * 1.5
    base_axis, base_diagonal = base * (1.0 / 18.0), base * (1.0 / 36.0)
    post = [base * (1.0 / 3.0) + solid * f[0]] + [None] * 18

    def put(i, even, odd):
        post[i] = (even + odd) + solid * f[i + 1]
        post[i + 1] = (even - odd) + solid * f[i]

    for i, square, h in ((1, xx, hx), (3, yy, hy), (5, zz, hz)):
        put(i, base_axis + 0.25 * square, 2.0 * h)
    for i, h, v in (
        (7, hx + hy, vx + vy),
        (9, hx - hy, vx - vy),
        (11, hx + hz, vx + vz),
        (13, hx - hz, vx - vz),
        (15, hy + hz, vy + vz),
        (17, hy - hz, vy - vz),
    ):
        put(i, base_diagonal + h * v, h)
    return post


def partner_devices():
    here_x, here_y = lax.axis_index("gx"), lax.axis_index("gy")
    along_x, along_y = lax.axis_size("gx"), lax.axis_size("gy")
    ahead_x, behind_x = lax.rem(here_x + 1, along_x), lax.rem(here_x + along_x - 1, along_x)
    ahead_y, behind_y = lax.rem(here_y + 1, along_y), lax.rem(here_y + along_y - 1, along_y)
    return (
        (ahead_x, here_y),
        (behind_x, here_y),
        (here_x, ahead_y),
        (here_x, behind_y),
        (ahead_x, ahead_y),
        (behind_x, behind_y),
        (ahead_x, behind_y),
        (behind_x, ahead_y),
    )


SIDE = {2: 0, 4: 0, 7: 0, 3: 1, 5: 1, 6: 1}
HALO_WAYS = ((2, 4, 7), (3, 6, 5))


def start_copy(way, partners, x_send, x_recv, y_send, y_recv, sent, came):
    if way < 2:
        source, landing = x_send.at[way], x_recv.at[way]
    else:
        source, landing = y_send.at[SIDE[way]], y_recv.at[way - 2]
    return pltpu.make_async_remote_copy(
        src_ref=source, dst_ref=landing, send_sem=sent.at[way], recv_sem=came.at[way],
        device_id=partners[way], device_id_type=MESH,
    )


def solid_copy(way, partners, solid, y_send, y_recv, sent, came):
    if way == 0:
        source, landing = solid.at[pl.ds(9, NEAR)], solid.at[pl.ds(1, NEAR)]
    elif way == 1:
        source, landing = solid.at[pl.ds(WIDE, NEAR)], solid.at[pl.ds(8 + WIDE, NEAR)]
    else:
        source, landing = y_send.at[SIDE[way]], y_recv.at[way - 2]
    return pltpu.make_async_remote_copy(
        src_ref=source, dst_ref=landing, send_sem=sent.at[way], recv_sem=came.at[way],
        device_id=partners[way], device_id_type=MESH,
    )


def pack_start(start, x_send, y_send):
    def population(number, carry):
        for way, first in ((0, 8 - NEAR), (1, 0)):
            for plane in range(NEAR):
                for half in range(2):
                    rows = start[number, pl.ds(128 * half + first + plane, 16, stride=8), :]
                    x_send[way, plane, number, 16 * half : 16 * half + 16, :] = rows.astype(jnp.bfloat16)
        y_send[0, number] = start[number, 8 * ROWS - 16 : 8 * ROWS, :].astype(jnp.bfloat16)
        y_send[1, number] = start[number, 0:16, :].astype(jnp.bfloat16)
        return carry

    lax.fori_loop(0, POPS, population, 0)


def reader(source, plane, tile):
    base = TOP + 8 * tile
    return lambda number, shift_x, down: source[plane - shift_x, number, base + down : base + down + 8, :]


def lattice(
    start, solid, even_posts, partners, odd_posts, even_stage, odd_stage, fx_send, fx_recv, fy_send, fy_recv, f_sent, f_came,
    sy_send, sy_recv, s_sent, s_came, f_edge, s_edge, far_send, far_recv, far_sent, far_came,
):
    posts = (even_posts, odd_posts)

    def start_halo(way):
        return start_copy(way, partners, fx_send, fx_recv, fy_send, fy_recv, f_sent, f_came)

    def solid_halo(way):
        return solid_copy(way, partners, solid, sy_send, sy_recv, s_sent, s_came)

    for way in range(8):
        solid_halo(way).start()

    def begin(plane, carry):
        for tile in range(4):
            f = [start[i, pl.ds(64 * tile + plane, 8, stride=8), :] for i in range(POPS)]
            post = collide(f, solid[plane + WIDE, 8 * tile : 8 * tile + 8, :])
            for i in range(POPS):
                posts[0][plane + WIDE, i, TOP + 8 * tile : TOP + 8 * tile + 8, :] = post[i]
        return carry

    def fetch(step, plane, tiles, stage):
        for tile in tiles:
            f = pull_all(reader(posts[(step - 1) % 2], plane, tile))
            for i in range(POPS):
                stage[tile, i] = f[i]

    def settle(step, plane, tiles, stage):
        for tile in tiles:
            post = collide([stage[tile, i] for i in range(POPS)], solid[plane, 8 * tile : 8 * tile + 8, :])
            for i in range(POPS):
                posts[step % 2][plane, i, TOP + 8 * tile : TOP + 8 * tile + 8, :] = post[i]

    def planes_of(step, first, last, tiles):
        def body(pair, carry):
            plane = first + 2 * pair
            fetch(step, plane + 1, tiles, odd_stage)
            settle(step, plane, tiles, even_stage)
            fetch(step, jnp.minimum(plane + 2, last - 1), tiles, even_stage)
            settle(step, plane + 1, tiles, odd_stage)
            return carry

        fetch(step, first, tiles, even_stage)
        lax.fori_loop(0, (last - first) // 2, body, 0)
        if (last - first) % 2:
            settle(step, last - 1, tiles, even_stage)

    def flat(step):
        return posts[step % 2].reshape(PLANES * POPS * TALL, LANES)

    def edge_rows(row, plane, number):
        return pl.ds((plane * POPS + number) * TALL + row, 8, stride=POPS * TALL)

    def edge(step, row, first):
        source, landing = flat(step - 1), flat(step)
        f = pull_all(lambda number, shift_x, down: source[edge_rows(row + down, first - shift_x, number), :])
        post = collide(f, s_edge[1 if row < TOP else 2, first : first + 8, :])
        for i in range(POPS):
            landing[edge_rows(row, first, i), :] = post[i]

    def far_copy(way):
        return pltpu.make_async_remote_copy(
            src_ref=far_send.at[way], dst_ref=far_recv.at[way], send_sem=far_sent.at[way], recv_sem=far_came.at[way],
            device_id=partners[way], device_id_type=MESH,
        )

    lax.fori_loop(0, 2, lambda side, carry: begin(8 - WIDE - side * (8 - 2 * WIDE + 1), carry), 0)
    for way, plane, group in ((0, 8, RIGHT), (1, 2 * WIDE - 1, LEFT)):
        for place, number in enumerate(group):
            for half in range(2):
                rows = posts[0][plane, number, TOP + 16 * half : TOP + 16 * half + 16, :]
                at = place * ROWS + 16 * half
                far_send[way, at : at + 16, :] = rows.astype(jnp.bfloat16)
        far_copy(way).start()
    lax.fori_loop(0, 6, lambda place, carry: begin(place + lax.div(place, 2), carry), 0)
    planes_of(1, 4, 10, (1, 2))

    for way in range(8):
        start_halo(way).wait_recv()

    def spread(number, carry):
        for side, ways in enumerate(HALO_WAYS):
            middle, below, above = [fy_recv[way - 2, number].astype(jnp.float32) for way in ways]
            for pair in range(2):
                f_edge[number, 2 * side + pair, WIDE : WIDE + 8, :] = middle[8 * pair : 8 * pair + 8]
                f_edge[number, 2 * side + pair, 0:WIDE, :] = below[8 * pair + 8 - WIDE : 8 * pair + 8]
                f_edge[number, 2 * side + pair, WIDE + 8 : PLANES, :] = above[8 * pair : 8 * pair + WIDE]
        return carry

    lax.fori_loop(0, POPS, spread, 0)
    for way in range(8):
        solid_halo(way).wait_recv()
    for side, ways in enumerate(HALO_WAYS):
        middle, below, above = [sy_recv[way - 2] for way in ways]
        for pair in range(2):
            s_edge[2 * side + pair, WIDE : WIDE + 8, :] = middle[8 * pair : 8 * pair + 8]
            s_edge[2 * side + pair, 0:WIDE, :] = below[8 * pair + 8 - WIDE : 8 * pair + 8]
            s_edge[2 * side + pair, WIDE + 8 : PLANES, :] = above[8 * pair : 8 * pair + WIDE]

    def begin_beside(plane, carry):
        for side in range(2):
            at = plane + (1 if side == 0 else 8 + WIDE)
            for half in range(2):
                f = [fx_recv[side, plane, i, 16 * half : 16 * half + 16, :].astype(jnp.float32) for i in range(POPS)]
                post = collide(f, solid[at, 16 * half : 16 * half + 16, :])
                for i in range(POPS):
                    posts[0][at, i, TOP + 16 * half : TOP + 16 * half + 16, :] = post[i]
        return carry

    lax.fori_loop(0, NEAR, begin_beside, 0)
    for way, plane, group in ((0, 0, RIGHT), (1, PLANES - 1, LEFT)):
        far_copy(way).wait_recv()
        for place, number in enumerate(group):
            for half in range(2):
                at = place * ROWS + 16 * half
                rows = far_recv[way, at : at + 16, :]
                posts[0][plane, number, TOP + 16 * half : TOP + 16 * half + 16, :] = rows.astype(jnp.float32)
    for place, row in enumerate((TOP - 2, TOP - 1, TOP + ROWS, TOP + ROWS + 1)):
        for first in (0, PLANES - 8):
            f = [f_edge[i, place, first : first + 8, :] for i in range(POPS)]
            post = collide(f, s_edge[place, first : first + 8, :])
            for i in range(POPS):
                flat(0)[edge_rows(row, first, i), :] = post[i]
    planes_of(1, 1, 4, range(4))
    planes_of(1, 10, 13, range(4))
    planes_of(1, 4, 10, (0, 3))
    for row in (TOP - 1, TOP + ROWS):
        for first in (1, 5):
            edge(1, row, first)
    planes_of(2, 2, 12, range(4))
    for row in (TOP - 1, TOP + ROWS):
        for first in (2, 4):
            edge(2, row, first)

    for way in range(8):
        start_halo(way).wait_send()
        solid_halo(way).wait_send()
    for way in range(2):
        far_copy(way).wait_send()


def lattice_scratch():
    return [
        pltpu.VMEM((PLANES, POPS, TALL, LANES), jnp.float32),
        pltpu.VMEM((4, POPS, 8, LANES), jnp.float32),
        pltpu.VMEM((4, POPS, 8, LANES), jnp.float32),
        pltpu.VMEM((2, NEAR, POPS, ROWS, LANES), jnp.bfloat16),
        pltpu.VMEM((2, NEAR, POPS, ROWS, LANES), jnp.bfloat16),
        pltpu.VMEM((2, POPS, 16, LANES), jnp.bfloat16),
        pltpu.VMEM((6, POPS, 16, LANES), jnp.bfloat16),
        pltpu.SemaphoreType.DMA((8,)),
        pltpu.SemaphoreType.DMA((8,)),
        pltpu.VMEM((2, 16, LANES), jnp.float32),
        pltpu.VMEM((6, 16, LANES), jnp.float32),
        pltpu.SemaphoreType.DMA((8,)),
        pltpu.SemaphoreType.DMA((8,)),
        pltpu.VMEM((POPS, 4, 16, LANES), jnp.float32),
        pltpu.VMEM((4, 16, LANES), jnp.float32),
        pltpu.VMEM((2, 5 * ROWS, LANES), jnp.bfloat16),
        pltpu.VMEM((2, 5 * ROWS, LANES), jnp.bfloat16),
        pltpu.SemaphoreType.DMA((2,)),
        pltpu.SemaphoreType.DMA((2,)),
    ]


def brick_slots(me, bricks, target_ref, count_ref, cell_ref, weight_ref, operand):
    blocks, nodes = cell_ref.shape
    row = lax.broadcasted_iota(jnp.int32, (blocks, blocks), 0)
    col = lax.broadcasted_iota(jnp.int32, (blocks, blocks), 1)
    target_row = target_ref[...].astype(jnp.float32)
    target_col = jnp.sum(jnp.where(row == col, target_row, 0.0), axis=1, keepdims=True)
    brick = lax.broadcasted_iota(jnp.int32, (blocks, bricks), 1)
    matches = jnp.where(brick.astype(jnp.float32) == target_col, 1.0, 0.0)
    before = jnp.where(col < row, 1.0, 0.0).astype(jnp.bfloat16)
    earlier = jnp.dot(before, matches.astype(jnp.bfloat16), preferred_element_type=jnp.float32)
    rank = jnp.sum(earlier * matches, axis=1, keepdims=True)
    slot_col = target_col * CAP + rank
    slot_row = jnp.sum(jnp.where(row == col, slot_col, 0.0), axis=0, keepdims=True)
    count_row = count_ref[...].astype(jnp.float32).reshape(1, blocks)
    count_col = jnp.sum(jnp.where(row == col, count_row, 0.0), axis=1, keepdims=True)
    node = lax.broadcasted_iota(jnp.int32, (blocks, nodes), 1).astype(jnp.float32)
    live = node < count_col
    cell = cell_ref[...]
    high = cell >> 7
    low = cell & 127
    weight = jnp.where(live, weight_ref[...].astype(jnp.float32), 0.0)
    for part in range(2):
        lanes = slice(part * LANES, (part + 1) * LANES)
        for number, values in enumerate((high.astype(jnp.float32), low.astype(jnp.float32), weight)):
            at = (part * 3 + number) * LANES
            operand[:, at : at + LANES] = values[:, lanes].astype(jnp.bfloat16)
    return slot_row


def gather_slots(me, bricks, slot_row, operand, outgoing):
    rows = CHUNK * 8
    place = lax.broadcasted_iota(jnp.int32, (rows, 1), 0)

    def chunk_of(chunk, carry):
        offset = chunk * CHUNK + (place >> 3)
        wanted = lax.rem(me + offset, bricks) * CAP + (place & (CAP - 1))
        pick = jnp.where(wanted.astype(jnp.float32) == slot_row, 1.0, 0.0).astype(jnp.bfloat16)
        found = jnp.dot(pick, operand[...], preferred_element_type=jnp.float32)
        lower = (place & 7) < CAP
        high, low, weight = [
            jnp.where(
                lower,
                found[:, number * LANES : (number + 1) * LANES],
                found[:, (3 + number) * LANES : (4 + number) * LANES],
            )
            for number in range(3)
        ]
        packed = ((weight * WEIGHT_STEPS).astype(jnp.int32) << 15) + (high * LANES + low).astype(jnp.int32)
        base = pl.multiple_of(chunk * CHUNK, CHUNK)
        outgoing[pl.ds(base, CHUNK)] = packed.reshape(CHUNK, 8, LANES)
        return carry

    lax.fori_loop(0, bricks // CHUNK, chunk_of, 0)


def device_at(me, step, bricks, along_y):
    target = lax.rem(me + step, bricks)
    return lax.div(target, along_y), lax.rem(target, along_y)


def one_hots(values, line):
    node = values[line : line + 1, :]
    high = (node >> 7) & 255
    low = node & 127
    weight = (node >> 15).astype(jnp.float32) * (1.0 / WEIGHT_STEPS)
    coarse = weight.astype(NARROW).astype(jnp.float32)
    rest = (weight - coarse) * REST_SCALE

    def wide(entry):
        return jnp.broadcast_to(entry.astype(jnp.float32), (16, LANES)).astype(jnp.bfloat16)

    high, low, coarse, rest = wide(high), wide(low), wide(coarse), wide(rest)
    counting = lax.broadcasted_iota(jnp.int32, (16, LANES), 0).astype(jnp.float32)
    one, zero = jnp.ones((16, LANES), jnp.bfloat16), jnp.zeros((16, LANES), jnp.bfloat16)
    rows, first, second = [], [], []
    for part in range(16):
        rows.append(jnp.where(high == (counting + 16 * part).astype(jnp.bfloat16), one, zero))
    for part in range(8):
        hit = low == (counting + 16 * part).astype(jnp.bfloat16)
        first.append(jnp.where(hit, coarse, zero))
        second.append(jnp.where(hit, rest, zero))
    return (
        jnp.concatenate(rows, 0).astype(NARROW),
        jnp.concatenate(first + second, 0).astype(NARROW),
    )


def program_kernel(
    bricks, along_y, target_hbm, count_hbm, cell_hbm, weight_hbm, start_hbm, solid_ref, even_posts,
    target_ref, count_ref, cell_ref, weight_ref, start, operand, outgoing, arrived, total, solid,
    load_sem, sent_sem, arrived_sem, *lattice_refs,
):
    fx_send, fx_recv, fy_send, fy_recv, f_sent, f_came, sy_send = lattice_refs[3:10]
    partners = partner_devices()
    me = lax.axis_index("gx") * along_y + lax.axis_index("gy")
    sources = (target_hbm, count_hbm, cell_hbm, weight_hbm, start_hbm)
    landings = (target_ref, count_ref, cell_ref, weight_ref, start)
    loads = [
        pltpu.make_async_copy(source, landing, load_sem.at[number])
        for number, (source, landing) in enumerate(zip(sources, landings))
    ]
    for load in loads:
        load.start()
    barrier = pltpu.get_barrier_semaphore()

    def greet(step, carry):
        pl.semaphore_signal(
            barrier, inc=1, device_id=device_at(me, step, bricks, along_y), device_id_type=MESH
        )
        return carry

    lax.fori_loop(1, bricks, greet, 0)
    for load in loads[:4]:
        load.wait()
    slot_row = brick_slots(me, bricks, target_ref, count_ref, cell_ref, weight_ref, operand)
    gather_slots(me, bricks, slot_row, operand, outgoing)
    loads[4].wait()
    pack_start(start, fx_send, fy_send)
    total[...] = jnp.zeros_like(total)
    pl.semaphore_wait(barrier, bricks - 1)

    def send(step, carry):
        pltpu.make_async_remote_copy(
            src_ref=outgoing.at[step],
            dst_ref=arrived.at[step],
            send_sem=sent_sem,
            recv_sem=arrived_sem.at[lax.div(step, GROUP)],
            device_id=device_at(me, step, bricks, along_y),
            device_id_type=MESH,
        ).start()
        return carry

    lax.fori_loop(1, bricks, send, 0)
    arrived[0] = outgoing[0]

    def add(group):
        left, right = [], []
        for member in range(GROUP):
            values = arrived[group * GROUP + member]
            for line in range(8):
                rows, columns = one_hots(values, line)
                left.append(rows)
                right.append(columns)
        total[...] += lax.dot_general(
            jnp.concatenate(left, 1),
            jnp.concatenate(right, 1),
            (((1,), (1,)), ((), ())),
            preferred_element_type=jnp.float32,
        )

    def landed(group, skip):
        whole = arrived.at[pl.ds(group * GROUP + skip, GROUP - skip)]
        pltpu.make_async_copy(whole, whole, arrived_sem.at[group]).wait()

    def later(group, carry):
        @pl.when(group == 0)
        def _():
            landed(0, 1)

        @pl.when(group > 0)
        def _():
            landed(group, 0)

        @pl.when(group == 0)
        def _():
            for way in range(8):
                start_copy(way, partners, fx_send, fx_recv, fy_send, fy_recv, f_sent, f_came).start()

        add(group)
        return carry

    lax.fori_loop(0, bricks // GROUP, later, 0)
    density = total[:, :LANES] + total[:, LANES:] * (1.0 / REST_SCALE)
    fraction = density / (1.0 + density)
    for plane in range(8):
        for tile in range(4):
            piece = fraction[plane * ROWS + 8 * tile : plane * ROWS + 8 * tile + 8, :]
            solid[plane + WIDE, 8 * tile : 8 * tile + 8, :] = piece
            solid_ref[pl.ds(64 * tile + plane, 8, stride=8), :] = piece
    sy_send[0] = solid_ref[8 * ROWS - 16 : 8 * ROWS, :]
    sy_send[1] = solid_ref[0:16, :]
    lattice(start, solid, even_posts, partners, *lattice_refs)
    everything = outgoing.at[pl.ds(1, bricks - 1)]
    pltpu.make_async_copy(everything, everything, sent_sem).wait()


def stream_out_kernel(posts, solid_ref, result_hbm, solid_hbm, result, out_sem, solid_sem):
    passing = pltpu.make_async_copy(solid_ref, solid_hbm, solid_sem)
    passing.start()

    def leave(tile):
        rows = pl.ds(64 * tile, 64)
        return pltpu.make_async_copy(result.at[:, rows], result_hbm.at[:, rows], out_sem.at[tile])

    for tile in range(4):

        def planes(pair, carry):
            for plane in (2 * pair, 2 * pair + 1):
                at = pl.ds(64 * tile + plane, 8, stride=8)
                for number, values in enumerate(pull_all(reader(posts, plane + WIDE, tile))):
                    result[number, at, :] = values
            return carry

        lax.fori_loop(0, 4, planes, 0)
        leave(tile).start()
    for tile in range(4):
        leave(tile).wait()
    passing.wait()


def stream_out(posts, solid):
    vmem, hbm = pl.BlockSpec(memory_space=pltpu.VMEM), pl.BlockSpec(memory_space=pltpu.HBM)
    shape = jax.ShapeDtypeStruct((POPS, 8 * ROWS, LANES), jnp.float32)
    return pl.pallas_call(
        stream_out_kernel,
        out_shape=(shape, jax.ShapeDtypeStruct(solid.shape, jnp.float32)),
        in_specs=[vmem, vmem],
        out_specs=(hbm, hbm),
        scratch_shapes=[
            pltpu.VMEM(shape.shape, jnp.float32), pltpu.SemaphoreType.DMA((4,)), pltpu.SemaphoreType.DMA
        ],
        compiler_params=pltpu.CompilerParams(vmem_limit_bytes=16 * 1024 * 1024),
        name="stream_out",
    )(pltpu.with_memory_space_constraint(posts, pltpu.VMEM), pltpu.with_memory_space_constraint(solid, pltpu.VMEM))


def to_rows(values):
    lead = values.shape[:-2]
    return jnp.swapaxes(values.reshape(lead + (8, ROWS, LANES)), -3, -2).reshape(lead + (8 * ROWS, LANES))


def from_rows(values):
    lead = values.shape[:-2]
    return jnp.swapaxes(values.reshape(lead + (ROWS, 8, LANES)), -3, -2).reshape(lead + (8, ROWS * LANES))


def on_device(populations, node_cell, node_weight, node_count, block_brick):
    along_y = lax.axis_size("gy")
    bricks = lax.axis_size("gx") * along_y
    blocks, nodes = node_cell.shape
    vmem, hbm = pl.BlockSpec(memory_space=pltpu.VMEM), pl.BlockSpec(memory_space=pltpu.HBM)
    solid, posts = pl.pallas_call(
        functools.partial(program_kernel, bricks, along_y),
        out_shape=(
            pltpu.VMEM((8 * ROWS, LANES), jnp.float32),
            pltpu.VMEM((PLANES, POPS, TALL, LANES), jnp.float32),
        ),
        in_specs=[hbm] * 5,
        out_specs=(vmem, vmem),
        scratch_shapes=[
            pltpu.VMEM((1, blocks), jnp.int32),
            pltpu.VMEM((blocks,), jnp.int32),
            pltpu.VMEM((blocks, nodes), jnp.int32),
            pltpu.VMEM((blocks, nodes), jnp.bfloat16),
            pltpu.VMEM((POPS, 8 * ROWS, LANES), jnp.float32),
            pltpu.VMEM((blocks, 6 * LANES), jnp.bfloat16),
            pltpu.VMEM((bricks, 8, LANES), jnp.int32),
            pltpu.VMEM((bricks, 8, LANES), jnp.int32),
            pltpu.VMEM((8 * ROWS, 2 * LANES), jnp.float32),
            pltpu.VMEM((PLANES, ROWS, LANES), jnp.float32),
            pltpu.SemaphoreType.DMA((5,)),
            pltpu.SemaphoreType.DMA,
            pltpu.SemaphoreType.DMA((bricks // GROUP,)),
        ]
        + lattice_scratch(),
        compiler_params=pltpu.CompilerParams(
            collective_id=0, has_side_effects=True, vmem_limit_bytes=40 * 1024 * 1024
        ),
        name="permeability",
    )(
        *(
            pltpu.with_memory_space_constraint(operand, pltpu.HBM)
            for operand in (
                block_brick.reshape(1, blocks), node_count, node_cell, node_weight, to_rows(populations)
            )
        )
    )
    result, solid = stream_out(posts, solid)
    return (from_rows(result), from_rows(solid))


def solution(mesh):
    return jax.shard_map(
        on_device,
        mesh=mesh,
        in_specs=(
            P(None, "gx", "gy"),
            P(("gx", "gy"), None),
            P(("gx", "gy"), None),
            P(("gx", "gy")),
            P(("gx", "gy"), None),
        ),
        out_specs=(P(None, "gx", "gy"), P("gx", "gy")),
        check_vma=False,
    )
```

```python
import functools

import jax
import jax.numpy as jnp
import numpy as np
from jax import lax
from jax.experimental import pallas as pl
from jax.experimental.pallas import tpu as pltpu
from jax.sharding import PartitionSpec as P

NZ = 64
STEPS = 3
CAP = 4
LANES = 128
GROUP = 16
CHUNK = 16
WEIGHT_STEPS = 1024.0
REST_SCALE = 64.0
MESH = pl.DeviceIdType.MESH
NARROW = jnp.float8_e4m3fn


lattice_velocities = (
    (0, 0, 0),
    (1, 0, 0),
    (-1, 0, 0),
    (0, 1, 0),
    (0, -1, 0),
    (0, 0, 1),
    (0, 0, -1),
    (1, 1, 0),
    (-1, -1, 0),
    (1, -1, 0),
    (-1, 1, 0),
    (1, 0, 1),
    (-1, 0, -1),
    (1, 0, -1),
    (-1, 0, 1),
    (0, 1, 1),
    (0, -1, -1),
    (0, 1, -1),
    (0, -1, 1),
)
opposite_of = (0, 2, 1, 4, 3, 6, 5, 8, 7, 10, 9, 12, 11, 14, 13, 16, 15, 18, 17)
lattice_weights = (1.0 / 3.0,) + (1.0 / 18.0,) * 6 + (1.0 / 36.0,) * 12


ROWS = 32
TOP = 8
TALL = 48
POPS = 19
RIGHT = (1, 7, 9, 11, 13)
LEFT = (2, 8, 10, 12, 14)
WIDE = STEPS
NEAR = WIDE - 1
PLANES = 8 + 2 * WIDE


def pull(read, number):
    shift_x, shift_y, shift_z = lattice_velocities[number]
    lane = lax.broadcasted_iota(jnp.int32, (8, LANES), 1)
    even, z_place = lane < NZ, lane & (NZ - 1)
    values = read(number, shift_x, 0)
    turn = 0
    if shift_y == 1:
        values = jnp.where(even, values, read(number, shift_x, -1))
        turn = NZ
    if shift_y == -1:
        values = jnp.where(even, read(number, shift_x, 1), values)
        turn = NZ
    if shift_z == 0:
        return pltpu.roll(values, turn, 1) if turn else values
    near = pltpu.roll(values, (shift_z + turn) % LANES, 1)
    wrapped = pltpu.roll(values, (shift_z + NZ + turn) % LANES, 1)
    return jnp.where(z_place == (0 if shift_z == 1 else NZ - 1), wrapped, near)


def pull_pair(read, number):
    return [pull(read, number), pull(read, number + 1)]


def pull_all(read):
    return [pull(read, number) for number in range(POPS)]


def collide(f, solid):
    pairs = range(1, POPS, 2)
    sums = {i: f[i] + f[i + 1] for i in pairs}
    diffs = {i: f[i] - f[i + 1] for i in pairs}
    rho = f[0] + ((sums[1] + sums[3]) + (sums[5] + sums[7])) + (
        ((sums[9] + sums[11]) + (sums[13] + sums[15])) + sums[17]
    )
    jx = (diffs[1] + diffs[7]) + (diffs[9] + diffs[11]) + diffs[13]
    jy = (diffs[3] + diffs[7]) + (diffs[15] + diffs[17]) - diffs[9]
    jz = (diffs[5] + diffs[11]) + (diffs[15] - diffs[13]) - diffs[17]
    fluid = 1.0 - solid
    inverse = 1.0 / rho
    ux, uy, uz = jx * inverse, jy * inverse, jz * inverse
    jx, jy, jz = jx * fluid, jy * fluid, jz * fluid
    xx, yy, zz = jx * ux, jy * uy, jz * uz
    base = rho * fluid - 1.5 * (xx + yy + zz)
    hx, hy, hz = jx * (1.0 / 12.0), jy * (1.0 / 12.0), jz * (1.0 / 12.0)
    vx, vy, vz = ux * 1.5, uy * 1.5, uz * 1.5
    base_axis, base_diagonal = base * (1.0 / 18.0), base * (1.0 / 36.0)
    post = [base * (1.0 / 3.0) + solid * f[0]] + [None] * 18

    def put(i, even, odd):
        post[i] = (even + odd) + solid * f[i + 1]
        post[i + 1] = (even - odd) + solid * f[i]

    for i, square, h in ((1, xx, hx), (3, yy, hy), (5, zz, hz)):
        put(i, base_axis + 0.25 * square, 2.0 * h)
    for i, h, v in (
        (7, hx + hy, vx + vy),
        (9, hx - hy, vx - vy),
        (11, hx + hz, vx + vz),
        (13, hx - hz, vx - vz),
        (15, hy + hz, vy + vz),
        (17, hy - hz, vy - vz),
    ):
        put(i, base_diagonal + h * v, h)
    return post


def partner_devices():
    here_x, here_y = lax.axis_index("gx"), lax.axis_index("gy")
    along_x, along_y = lax.axis_size("gx"), lax.axis_size("gy")
    ahead_x, behind_x = lax.rem(here_x + 1, along_x), lax.rem(here_x + along_x - 1, along_x)
    ahead_y, behind_y = lax.rem(here_y + 1, along_y), lax.rem(here_y + along_y - 1, along_y)
    return (
        (ahead_x, here_y),
        (behind_x, here_y),
        (here_x, ahead_y),
        (here_x, behind_y),
        (ahead_x, ahead_y),
        (behind_x, behind_y),
        (ahead_x, behind_y),
        (behind_x, ahead_y),
    )


SIDE = {2: 0, 4: 0, 7: 0, 3: 1, 5: 1, 6: 1}
HALO_WAYS = ((2, 4, 7), (3, 6, 5))


def start_copy(way, partners, x_send, x_recv, y_send, y_recv, sent, came):
    if way < 2:
        source, landing = x_send.at[way], x_recv.at[way]
    else:
        source, landing = y_send.at[SIDE[way]], y_recv.at[way - 2]
    return pltpu.make_async_remote_copy(
        src_ref=source, dst_ref=landing, send_sem=sent.at[way], recv_sem=came.at[way],
        device_id=partners[way], device_id_type=MESH,
    )


def solid_copy(way, partners, solid, y_send, y_recv, sent, came):
    if way == 0:
        source, landing = solid.at[pl.ds(9, NEAR)], solid.at[pl.ds(1, NEAR)]
    elif way == 1:
        source, landing = solid.at[pl.ds(WIDE, NEAR)], solid.at[pl.ds(8 + WIDE, NEAR)]
    else:
        source, landing = y_send.at[SIDE[way]], y_recv.at[way - 2]
    return pltpu.make_async_remote_copy(
        src_ref=source, dst_ref=landing, send_sem=sent.at[way], recv_sem=came.at[way],
        device_id=partners[way], device_id_type=MESH,
    )


def pack_start(start, x_send, y_send):
    def population(number, carry):
        for way, first in ((0, 8 - NEAR), (1, 0)):
            for plane in range(NEAR):
                for half in range(2):
                    rows = start[number, pl.ds(128 * half + first + plane, 16, stride=8), :]
                    x_send[way, plane, number, 16 * half : 16 * half + 16, :] = rows.astype(jnp.bfloat16)
        y_send[0, number] = start[number, 8 * ROWS - 16 : 8 * ROWS, :].astype(jnp.bfloat16)
        y_send[1, number] = start[number, 0:16, :].astype(jnp.bfloat16)
        return carry

    lax.fori_loop(0, POPS, population, 0)


def reader(source, plane, tile):
    base = TOP + 8 * tile
    return lambda number, shift_x, down: source[plane - shift_x, number, base + down : base + down + 8, :]


def lattice(
    start, solid, even_posts, partners, odd_posts, even_stage, odd_stage, fx_send, fx_recv, fy_send, fy_recv, f_sent, f_came,
    sy_send, sy_recv, s_sent, s_came, f_edge, s_edge, far_send, far_recv, far_sent, far_came,
):
    posts = (even_posts, odd_posts)

    def start_halo(way):
        return start_copy(way, partners, fx_send, fx_recv, fy_send, fy_recv, f_sent, f_came)

    def solid_halo(way):
        return solid_copy(way, partners, solid, sy_send, sy_recv, s_sent, s_came)

    for way in range(8):
        solid_halo(way).start()

    def begin(plane, carry):
        for tile in range(4):
            f = [start[i, pl.ds(64 * tile + plane, 8, stride=8), :] for i in range(POPS)]
            post = collide(f, solid[plane + WIDE, 8 * tile : 8 * tile + 8, :])
            for i in range(POPS):
                posts[0][plane + WIDE, i, TOP + 8 * tile : TOP + 8 * tile + 8, :] = post[i]
        return carry

    def fetch(step, plane, tiles, stage):
        for tile in tiles:
            f = pull_all(reader(posts[(step - 1) % 2], plane, tile))
            for i in range(POPS):
                stage[tile, i] = f[i]

    def settle(step, plane, tiles, stage):
        for tile in tiles:
            post = collide([stage[tile, i] for i in range(POPS)], solid[plane, 8 * tile : 8 * tile + 8, :])
            for i in range(POPS):
                posts[step % 2][plane, i, TOP + 8 * tile : TOP + 8 * tile + 8, :] = post[i]

    def planes_of(step, first, last, tiles):
        def body(pair, carry):
            plane = first + 2 * pair
            fetch(step, plane + 1, tiles, odd_stage)
            settle(step, plane, tiles, even_stage)
            fetch(step, jnp.minimum(plane + 2, last - 1), tiles, even_stage)
            settle(step, plane + 1, tiles, odd_stage)
            return carry

        fetch(step, first, tiles, even_stage)
        lax.fori_loop(0, (last - first) // 2, body, 0)
        if (last - first) % 2:
            settle(step, last - 1, tiles, even_stage)

    def flat(step):
        return posts[step % 2].reshape(PLANES * POPS * TALL, LANES)

    def edge_rows(row, plane, number):
        return pl.ds((plane * POPS + number) * TALL + row, 8, stride=POPS * TALL)

    def edge(step, row, first):
        source, landing = flat(step - 1), flat(step)
        f = pull_all(lambda number, shift_x, down: source[edge_rows(row + down, first - shift_x, number), :])
        post = collide(f, s_edge[1 if row < TOP else 2, first : first + 8, :])
        for i in range(POPS):
            landing[edge_rows(row, first, i), :] = post[i]

    def far_copy(way):
        return pltpu.make_async_remote_copy(
            src_ref=far_send.at[way], dst_ref=far_recv.at[way], send_sem=far_sent.at[way], recv_sem=far_came.at[way],
            device_id=partners[way], device_id_type=MESH,
        )

    lax.fori_loop(0, 2, lambda side, carry: begin(8 - WIDE - side * (8 - 2 * WIDE + 1), carry), 0)
    for way, plane, group in ((0, 8, RIGHT), (1, 2 * WIDE - 1, LEFT)):
        for place, number in enumerate(group):
            for half in range(2):
                rows = posts[0][plane, number, TOP + 16 * half : TOP + 16 * half + 16, :]
                at = place * ROWS + 16 * half
                far_send[way, at : at + 16, :] = rows.astype(jnp.bfloat16)
        far_copy(way).start()
    lax.fori_loop(0, 6, lambda place, carry: begin(place + lax.div(place, 2), carry), 0)
    planes_of(1, 4, 10, (1, 2))

    for way in range(8):
        start_halo(way).wait_recv()

    def spread(number, carry):
        for side, ways in enumerate(HALO_WAYS):
            middle, below, above = [fy_recv[way - 2, number].astype(jnp.float32) for way in ways]
            for pair in range(2):
                f_edge[number, 2 * side + pair, WIDE : WIDE + 8, :] = middle[8 * pair : 8 * pair + 8]
                f_edge[number, 2 * side + pair, 0:WIDE, :] = below[8 * pair + 8 - WIDE : 8 * pair + 8]
                f_edge[number, 2 * side + pair, WIDE + 8 : PLANES, :] = above[8 * pair : 8 * pair + WIDE]
        return carry

    lax.fori_loop(0, POPS, spread, 0)
    for way in range(8):
        solid_halo(way).wait_recv()
    for side, ways in enumerate(HALO_WAYS):
        middle, below, above = [sy_recv[way - 2] for way in ways]
        for pair in range(2):
            s_edge[2 * side + pair, WIDE : WIDE + 8, :] = middle[8 * pair : 8 * pair + 8]
            s_edge[2 * side + pair, 0:WIDE, :] = below[8 * pair + 8 - WIDE : 8 * pair + 8]
            s_edge[2 * side + pair, WIDE + 8 : PLANES, :] = above[8 * pair : 8 * pair + WIDE]

    def begin_beside(plane, carry):
        for side in range(2):
            at = plane + (1 if side == 0 else 8 + WIDE)
            for half in range(2):
                f = [fx_recv[side, plane, i, 16 * half : 16 * half + 16, :].astype(jnp.float32) for i in range(POPS)]
                post = collide(f, solid[at, 16 * half : 16 * half + 16, :])
                for i in range(POPS):
                    posts[0][at, i, TOP + 16 * half : TOP + 16 * half + 16, :] = post[i]
        return carry

    lax.fori_loop(0, NEAR, begin_beside, 0)
    for way, plane, group in ((0, 0, RIGHT), (1, PLANES - 1, LEFT)):
        far_copy(way).wait_recv()
        for place, number in enumerate(group):
            for half in range(2):
                at = place * ROWS + 16 * half
                rows = far_recv[way, at : at + 16, :]
                posts[0][plane, number, TOP + 16 * half : TOP + 16 * half + 16, :] = rows.astype(jnp.float32)
    for place, row in enumerate((TOP - 2, TOP - 1, TOP + ROWS, TOP + ROWS + 1)):
        for first in (0, PLANES - 8):
            f = [f_edge[i, place, first : first + 8, :] for i in range(POPS)]
            post = collide(f, s_edge[place, first : first + 8, :])
            for i in range(POPS):
                flat(0)[edge_rows(row, first, i), :] = post[i]
    planes_of(1, 1, 4, range(4))
    planes_of(1, 10, 13, range(4))
    planes_of(1, 4, 10, (0, 3))
    for row in (TOP - 1, TOP + ROWS):
        for first in (1, 5):
            edge(1, row, first)
    planes_of(2, 2, 12, range(4))
    for row in (TOP - 1, TOP + ROWS):
        for first in (2, 4):
            edge(2, row, first)

    for way in range(8):
        start_halo(way).wait_send()
        solid_halo(way).wait_send()
    for way in range(2):
        far_copy(way).wait_send()


def lattice_scratch():
    return [
        pltpu.VMEM((PLANES, POPS, TALL, LANES), jnp.float32),
        pltpu.VMEM((4, POPS, 8, LANES), jnp.float32),
        pltpu.VMEM((4, POPS, 8, LANES), jnp.float32),
        pltpu.VMEM((2, NEAR, POPS, ROWS, LANES), jnp.bfloat16),
        pltpu.VMEM((2, NEAR, POPS, ROWS, LANES), jnp.bfloat16),
        pltpu.VMEM((2, POPS, 16, LANES), jnp.bfloat16),
        pltpu.VMEM((6, POPS, 16, LANES), jnp.bfloat16),
        pltpu.SemaphoreType.DMA((8,)),
        pltpu.SemaphoreType.DMA((8,)),
        pltpu.VMEM((2, 16, LANES), jnp.float32),
        pltpu.VMEM((6, 16, LANES), jnp.float32),
        pltpu.SemaphoreType.DMA((8,)),
        pltpu.SemaphoreType.DMA((8,)),
        pltpu.VMEM((POPS, 4, 16, LANES), jnp.float32),
        pltpu.VMEM((4, 16, LANES), jnp.float32),
        pltpu.VMEM((2, 5 * ROWS, LANES), jnp.bfloat16),
        pltpu.VMEM((2, 5 * ROWS, LANES), jnp.bfloat16),
        pltpu.SemaphoreType.DMA((2,)),
        pltpu.SemaphoreType.DMA((2,)),
    ]


def brick_slots(bricks, target_ref, count_ref, cell_ref, weight_ref, operand):
    blocks, nodes = cell_ref.shape
    row = lax.broadcasted_iota(jnp.int32, (blocks, blocks), 0)
    col = lax.broadcasted_iota(jnp.int32, (blocks, blocks), 1)
    target_row = target_ref[...].astype(jnp.float32)
    target_col = jnp.sum(jnp.where(row == col, target_row, 0.0), axis=1, keepdims=True)
    brick = lax.broadcasted_iota(jnp.int32, (blocks, bricks), 1)
    matches = jnp.where(brick.astype(jnp.float32) == target_col, 1.0, 0.0)
    before = jnp.where(col < row, 1.0, 0.0).astype(jnp.bfloat16)
    earlier = jnp.dot(before, matches.astype(jnp.bfloat16), preferred_element_type=jnp.float32)
    rank = jnp.sum(earlier * matches, axis=1, keepdims=True)
    slot_col = target_col * CAP + rank
    slot_row = jnp.sum(jnp.where(row == col, slot_col, 0.0), axis=0, keepdims=True)
    count_row = count_ref[...].astype(jnp.float32).reshape(1, blocks)
    count_col = jnp.sum(jnp.where(row == col, count_row, 0.0), axis=1, keepdims=True)
    node = lax.broadcasted_iota(jnp.int32, (blocks, nodes), 1).astype(jnp.float32)
    live = node < count_col
    cell = cell_ref[...]
    high = cell >> 7
    low = cell & 127
    weight = jnp.where(live, weight_ref[...].astype(jnp.float32), 0.0)
    for part in range(2):
        lanes = slice(part * LANES, (part + 1) * LANES)
        for number, values in enumerate((high.astype(jnp.float32), low.astype(jnp.float32), weight)):
            at = (part * 3 + number) * LANES
            operand[:, at : at + LANES] = values[:, lanes].astype(jnp.bfloat16)
    return slot_row


def gather_slots(bricks, along_y, slot_row, operand, outgoing):
    rows = CHUNK * 8
    here_x, here_y = lax.axis_index("gx"), lax.axis_index("gy")
    place = lax.broadcasted_iota(jnp.int32, (rows, 1), 0)

    def chunk_of(chunk, carry):
        offset = chunk * CHUNK + (place >> 3)
        there_x = lax.rem(here_x + lax.div(offset, along_y), bricks // along_y)
        there_y = lax.rem(here_y + lax.rem(offset, along_y), along_y)
        wanted = (there_x * along_y + there_y) * CAP + (place & (CAP - 1))
        pick = jnp.where(wanted.astype(jnp.float32) == slot_row, 1.0, 0.0).astype(jnp.bfloat16)
        found = jnp.dot(pick, operand[...], preferred_element_type=jnp.float32)
        lower = (place & 7) < CAP
        high, low, weight = [
            jnp.where(
                lower,
                found[:, number * LANES : (number + 1) * LANES],
                found[:, (3 + number) * LANES : (4 + number) * LANES],
            )
            for number in range(3)
        ]
        packed = ((weight * WEIGHT_STEPS).astype(jnp.int32) << 15) + (high * LANES + low).astype(jnp.int32)
        base = pl.multiple_of(chunk * CHUNK, CHUNK)
        outgoing[pl.ds(base, CHUNK)] = packed.reshape(CHUNK, 8, LANES)
        return carry

    lax.fori_loop(0, bricks // CHUNK, chunk_of, 0)


def for_each_partner(along_x, along_y, act):
    here_x, here_y = lax.axis_index("gx"), lax.axis_index("gy")
    there_y = [lax.rem(here_y + turn, along_y) for turn in range(along_y)]

    def column(turn, carry):
        there_x = lax.rem(here_x + turn, along_x)
        for place in range(along_y):
            act(turn * along_y + place, turn, (there_x, there_y[place]))
        return carry

    for place in range(1, along_y):
        act(place, 0, (here_x, there_y[place]))
    lax.fori_loop(1, along_x, column, 0)


def one_hots(values, line):
    node = values[line : line + 1, :]
    high = (node >> 7) & 255
    low = node & 127
    weight = (node >> 15).astype(jnp.float32) * (1.0 / WEIGHT_STEPS)
    coarse = weight.astype(NARROW).astype(jnp.float32)
    rest = (weight - coarse) * REST_SCALE

    def wide(entry):
        return jnp.broadcast_to(entry.astype(jnp.float32), (16, LANES)).astype(jnp.bfloat16)

    high, low, coarse, rest = wide(high), wide(low), wide(coarse), wide(rest)
    counting = lax.broadcasted_iota(jnp.int32, (16, LANES), 0).astype(jnp.float32)
    one, zero = jnp.ones((16, LANES), jnp.bfloat16), jnp.zeros((16, LANES), jnp.bfloat16)
    rows, first, second = [], [], []
    for part in range(16):
        rows.append(jnp.where(high == (counting + 16 * part).astype(jnp.bfloat16), one, zero))
    for part in range(8):
        hit = low == (counting + 16 * part).astype(jnp.bfloat16)
        first.append(jnp.where(hit, coarse, zero))
        second.append(jnp.where(hit, rest, zero))
    return (
        jnp.concatenate(rows, 0).astype(NARROW),
        jnp.concatenate(first + second, 0).astype(NARROW),
    )


def program_kernel(
    bricks, along_y, target_hbm, count_hbm, cell_hbm, weight_hbm, start_hbm, solid_ref, even_posts,
    target_ref, count_ref, cell_ref, weight_ref, start, operand, outgoing, arrived, total, solid,
    load_sem, sent_sem, arrived_sem, *lattice_refs,
):
    fx_send, fx_recv, fy_send, fy_recv, f_sent, f_came, sy_send = lattice_refs[3:10]
    partners = partner_devices()
    along_x = bricks // along_y
    sources = (target_hbm, count_hbm, cell_hbm, weight_hbm, start_hbm)
    landings = (target_ref, count_ref, cell_ref, weight_ref, start)
    loads = [
        pltpu.make_async_copy(source, landing, load_sem.at[number])
        for number, (source, landing) in enumerate(zip(sources, landings))
    ]
    for load in loads:
        load.start()
    barrier = pltpu.get_barrier_semaphore()

    def greet(step, turn, device):
        pl.semaphore_signal(barrier, inc=1, device_id=device, device_id_type=MESH)

    for_each_partner(along_x, along_y, greet)
    for load in loads[:4]:
        load.wait()
    slot_row = brick_slots(bricks, target_ref, count_ref, cell_ref, weight_ref, operand)
    gather_slots(bricks, along_y, slot_row, operand, outgoing)
    loads[4].wait()
    pack_start(start, fx_send, fy_send)
    total[...] = jnp.zeros_like(total)
    pl.semaphore_wait(barrier, bricks - 1)

    def send(step, turn, device):
        pltpu.make_async_remote_copy(
            src_ref=outgoing.at[step],
            dst_ref=arrived.at[step],
            send_sem=sent_sem,
            recv_sem=arrived_sem.at[lax.div(turn, GROUP // along_y)],
            device_id=device,
            device_id_type=MESH,
        ).start()

    for_each_partner(along_x, along_y, send)
    arrived[0] = outgoing[0]

    def add(group):
        left, right = [], []
        for member in range(GROUP):
            values = arrived[group * GROUP + member]
            for line in range(8):
                rows, columns = one_hots(values, line)
                left.append(rows)
                right.append(columns)
        total[...] += lax.dot_general(
            jnp.concatenate(left, 1),
            jnp.concatenate(right, 1),
            (((1,), (1,)), ((), ())),
            preferred_element_type=jnp.float32,
        )

    def landed(group, skip):
        whole = arrived.at[pl.ds(group * GROUP + skip, GROUP - skip)]
        pltpu.make_async_copy(whole, whole, arrived_sem.at[group]).wait()

    def later(group, carry):
        @pl.when(group == 0)
        def _():
            landed(0, 1)

        @pl.when(group > 0)
        def _():
            landed(group, 0)

        @pl.when(group == 0)
        def _():
            for way in range(8):
                start_copy(way, partners, fx_send, fx_recv, fy_send, fy_recv, f_sent, f_came).start()

        add(group)
        return carry

    lax.fori_loop(0, bricks // GROUP, later, 0)
    density = total[:, :LANES] + total[:, LANES:] * (1.0 / REST_SCALE)
    fraction = density / (1.0 + density)
    for plane in range(8):
        for tile in range(4):
            piece = fraction[plane * ROWS + 8 * tile : plane * ROWS + 8 * tile + 8, :]
            solid[plane + WIDE, 8 * tile : 8 * tile + 8, :] = piece
            solid_ref[pl.ds(64 * tile + plane, 8, stride=8), :] = piece
    sy_send[0] = solid_ref[8 * ROWS - 16 : 8 * ROWS, :]
    sy_send[1] = solid_ref[0:16, :]
    lattice(start, solid, even_posts, partners, *lattice_refs)
    everything = outgoing.at[pl.ds(1, bricks - 1)]
    pltpu.make_async_copy(everything, everything, sent_sem).wait()


def stream_out_kernel(posts, solid_ref, result_hbm, solid_hbm, result, out_sem, solid_sem):
    passing = pltpu.make_async_copy(solid_ref, solid_hbm, solid_sem)
    passing.start()

    def leave(tile):
        rows = pl.ds(64 * tile, 64)
        return pltpu.make_async_copy(result.at[:, rows], result_hbm.at[:, rows], out_sem.at[tile])

    for tile in range(4):

        def planes(pair, carry):
            for plane in (2 * pair, 2 * pair + 1):
                at = pl.ds(64 * tile + plane, 8, stride=8)
                for number, values in enumerate(pull_all(reader(posts, plane + WIDE, tile))):
                    result[number, at, :] = values
            return carry

        lax.fori_loop(0, 4, planes, 0)
        leave(tile).start()
    for tile in range(4):
        leave(tile).wait()
    passing.wait()


def stream_out(posts, solid):
    vmem, hbm = pl.BlockSpec(memory_space=pltpu.VMEM), pl.BlockSpec(memory_space=pltpu.HBM)
    shape = jax.ShapeDtypeStruct((POPS, 8 * ROWS, LANES), jnp.float32)
    return pl.pallas_call(
        stream_out_kernel,
        out_shape=(shape, jax.ShapeDtypeStruct(solid.shape, jnp.float32)),
        in_specs=[vmem, vmem],
        out_specs=(hbm, hbm),
        scratch_shapes=[
            pltpu.VMEM(shape.shape, jnp.float32), pltpu.SemaphoreType.DMA((4,)), pltpu.SemaphoreType.DMA
        ],
        compiler_params=pltpu.CompilerParams(vmem_limit_bytes=16 * 1024 * 1024),
        name="stream_out",
    )(pltpu.with_memory_space_constraint(posts, pltpu.VMEM), pltpu.with_memory_space_constraint(solid, pltpu.VMEM))


def to_rows(values):
    lead = values.shape[:-2]
    return jnp.swapaxes(values.reshape(lead + (8, ROWS, LANES)), -3, -2).reshape(lead + (8 * ROWS, LANES))


def from_rows(values):
    lead = values.shape[:-2]
    return jnp.swapaxes(values.reshape(lead + (ROWS, 8, LANES)), -3, -2).reshape(lead + (8, ROWS * LANES))


def on_device(populations, node_cell, node_weight, node_count, block_brick):
    along_y = lax.axis_size("gy")
    bricks = lax.axis_size("gx") * along_y
    blocks, nodes = node_cell.shape
    vmem, hbm = pl.BlockSpec(memory_space=pltpu.VMEM), pl.BlockSpec(memory_space=pltpu.HBM)
    solid, posts = pl.pallas_call(
        functools.partial(program_kernel, bricks, along_y),
        out_shape=(
            pltpu.VMEM((8 * ROWS, LANES), jnp.float32),
            pltpu.VMEM((PLANES, POPS, TALL, LANES), jnp.float32),
        ),
        in_specs=[hbm] * 5,
        out_specs=(vmem, vmem),
        scratch_shapes=[
            pltpu.VMEM((1, blocks), jnp.int32),
            pltpu.VMEM((blocks,), jnp.int32),
            pltpu.VMEM((blocks, nodes), jnp.int32),
            pltpu.VMEM((blocks, nodes), jnp.bfloat16),
            pltpu.VMEM((POPS, 8 * ROWS, LANES), jnp.float32),
            pltpu.VMEM((blocks, 6 * LANES), jnp.bfloat16),
            pltpu.VMEM((bricks, 8, LANES), jnp.int32),
            pltpu.VMEM((bricks, 8, LANES), jnp.int32),
            pltpu.VMEM((8 * ROWS, 2 * LANES), jnp.float32),
            pltpu.VMEM((PLANES, ROWS, LANES), jnp.float32),
            pltpu.SemaphoreType.DMA((5,)),
            pltpu.SemaphoreType.DMA,
            pltpu.SemaphoreType.DMA((bricks // GROUP,)),
        ]
        + lattice_scratch(),
        compiler_params=pltpu.CompilerParams(
            collective_id=0, has_side_effects=True, vmem_limit_bytes=40 * 1024 * 1024
        ),
        name="permeability",
    )(
        *(
            pltpu.with_memory_space_constraint(operand, pltpu.HBM)
            for operand in (
                block_brick.reshape(1, blocks), node_count, node_cell, node_weight, to_rows(populations)
            )
        )
    )
    result, solid = stream_out(posts, solid)
    return (from_rows(result), from_rows(solid))


def solution(mesh):
    return jax.shard_map(
        on_device,
        mesh=mesh,
        in_specs=(
            P(None, "gx", "gy"),
            P(("gx", "gy"), None),
            P(("gx", "gy"), None),
            P(("gx", "gy")),
            P(("gx", "gy"), None),
        ),
        out_specs=(P(None, "gx", "gy"), P("gx", "gy")),
        check_vma=False,
    )
```
